256 devices in a mesh: seq: 32 (over z, y), fsdp: 8 (over x, core).
Axes of the slice: x: 4, y: 4, z: 8, core: 2. Of those that a mesh axis runs over, the one named last changes fastest.
Arguments:
- queries: bfloat16 [32, 8, 256, 2560], P('seq', 'fsdp'), may hold values from -6 to 6
- key_rows: bfloat16 [32, 8, 256, 2560], P('seq', 'fsdp'), may hold values from -6 to 6
- value_rows: bfloat16 [32, 8, 256, 2560], P('seq', 'fsdp'), may hold values from -6 to 6
- cache_keys: bfloat16 [32, 4, 8, 64, 2560], P('seq', None, 'fsdp'), may hold values from -6 to 6
- cache_values: bfloat16 [32, 4, 8, 64, 2560], P('seq', None, 'fsdp'), may hold values from -6 to 6
- cache_frames: int32 [4, 8], P(None, 'fsdp'), may hold values from 1 to 8, as said below
- neighbors: int32 [32, 9], replicated, may hold values from 0 to 31, as said below
- tile_order: int32 [32], replicated, may hold values from 0 to 31, each once
- out_weight: bfloat16 [2560, 5120], P('fsdp', 'seq'), may hold values from -0.125 to 0.125
Outputs:
- block_output: bfloat16 [32, 8, 256, 5120], P('seq', 'fsdp')
The draws below stay inside these ranges and needn't reach their ends.
Inputs may be any that keep to these rules, and one draw needn't show every extreme that they name: The last cache_frames[b, g] of the 8 cache frames are live for trajectory (b, g); some trajectory has all 8, and the counts are not all equal. `neighbors`: row t names 9 different tiles of the frame, t itself first; tiles lie on a grid in rows of 8. `tile_order`: each tile stands in exactly one slot.
All inputs are finite; a program needn't handle non-finite values.
Results may differ from the reference program's by a relative error of at most 0.017.
Values may be sent and summed in bfloat16 or wider, within the bound.
A program may use at most 128 MiB of HBM per device.

```python
import jax
import jax.numpy as jnp
from jax import lax

D = 5120
HEADS = 20
HD = 128
TILE = 8
SPAN = 8
CACHE = 8
TILES = 32
TPG = 4
NB = 9
TOKF = 256
HH = 2560
N_FSDP = 8


def draw_queries(key, part):
    key = jax.random.fold_in(key, 11)
    shape = (TPG * SPAN, N_FSDP, TILES * TILE, HEADS * HD)
    base = jnp.clip(jax.random.normal(key, shape, jnp.float32), -6.0, 6.0)
    return base.astype(jnp.bfloat16)


def draw_key_rows(key, part):
    key = jax.random.fold_in(key, 13)
    shape = (TPG * SPAN, N_FSDP, TILES * TILE, HEADS * HD)
    base = jnp.clip(jax.random.normal(key, shape, jnp.float32), -6.0, 6.0)
    return base.astype(jnp.bfloat16)


def draw_cache_frames(key, part):
    key = jax.random.fold_in(key, 5)
    total = TPG * N_FSDP
    counts = jax.random.randint(key, (total,), 1, CACHE + 1)
    chosen = jax.random.randint(jax.random.fold_in(key, 1), (), 0, total)
    lower = jax.random.randint(jax.random.fold_in(key, 2), (), 1, CACHE)
    counts = counts.at[(chosen + 1) % total].set(lower)
    counts = counts.at[chosen].set(CACHE)
    return counts.reshape(TPG, N_FSDP).astype(jnp.int32)


def draw_neighbors(key, part):
    key = jax.random.fold_in(key, 7)
    ident = jnp.arange(TILES, dtype=jnp.int32)
    grid_row = ident // 8
    grid_col = ident % 8
    distance = jnp.maximum(jnp.abs(grid_row[:, None] - grid_row[None, :]), jnp.abs(grid_col[:, None] - grid_col[None, :]))
    jitter = jax.random.randint(jax.random.fold_in(key, 1), (TILES, TILES), 0, 2)
    noise = jax.random.randint(jax.random.fold_in(key, 2), (TILES, TILES), 0, 4096)
    score = ((distance + jitter) * 4096 + noise) * TILES + ident[None, :]
    score = jnp.where(ident[:, None] == ident[None, :], -1, score)
    chosen = lax.top_k(-score, NB)[1]
    return chosen.astype(jnp.int32)


def level_of(stream_key, dims, cuts, smallest, largest):
    def one(dim, parts):
        draws = jax.random.uniform(jax.random.fold_in(jax.random.fold_in(stream_key, 6), dim), (parts,), jnp.float32, smallest / len(cuts), largest / len(cuts))
        return jnp.repeat(jnp.exp(draws), dims[dim] // parts).reshape((-1,) + (1,) * (len(dims) - dim - 1))

    factor_of = one(*cuts[0])
    for cut in cuts[1:]:
        factor_of = factor_of * one(*cut)
    return factor_of


def gaussian(rng, dims, deviation, bound, cuts=(), kind=jnp.bfloat16):
    gain = level_of(rng, dims, cuts, -0.22, 0.18) if cuts else 1.0
    values = jax.random.normal(rng, dims, jnp.float32) * deviation * gain
    return jnp.minimum(jnp.maximum(values, -bound), bound).astype(kind)


def setup_inputs(seed: int = 0) -> dict:
    key_of = jax.random.split(jax.random.key(seed), 10)
    return {
        "queries": draw_queries(jax.random.fold_in(key_of[9], 71), 0),
        "key_rows": draw_key_rows(jax.random.fold_in(key_of[9], 71), 0),
        "value_rows": gaussian(key_of[2], (TPG * SPAN, N_FSDP, TOKF, HH), 1.0, 6.0, ((0, 32), (1, 8))),
        "cache_keys": gaussian(key_of[3], (TILES, TPG, N_FSDP, CACHE * TILE, HH), 1.0, 6.0, ((0, 32), (2, 8))),
        "cache_values": gaussian(key_of[4], (TILES, TPG, N_FSDP, CACHE * TILE, HH), 1.0, 6.0, ((0, 32), (2, 8))),
        "cache_frames": draw_cache_frames(jax.random.fold_in(key_of[9], 71), 0),
        "neighbors": draw_neighbors(jax.random.fold_in(key_of[9], 71), 0),
        "tile_order": jax.random.permutation(key_of[7], TILES).astype(jnp.int32),
        "out_weight": gaussian(key_of[8], (HH, D), HH ** -0.5, 0.125, ((0, 8), (1, 32))),
    }


def normalized(scores):
    top = jnp.max(scores, axis=-1, keepdims=True)
    weights = jnp.exp(scores - top)
    return (weights / jnp.sum(weights, axis=-1, keepdims=True)).astype(jnp.bfloat16)


def spatial_frame(frame_q, frame_k, frame_v, neighbors):
    near_k = frame_k[neighbors].reshape(TILES, NB * TILE, HEADS, HD)
    near_v = frame_v[neighbors].reshape(TILES, NB * TILE, HEADS, HD)
    scores = jnp.einsum("tihd,tjhd->thij", frame_q.astype(jnp.float32), near_k.astype(jnp.float32)) * (HD ** -0.5)
    probs = normalized(scores).astype(jnp.float32)
    return jnp.einsum("thij,tjhd->tihd", probs, near_v.astype(jnp.float32)).astype(jnp.bfloat16)


def temporal_slot(slot, tile, whole_q, whole_k, whole_v, cache_keys, cache_values, cache_frames):
    tile_q = lax.dynamic_index_in_dim(whole_q, tile, 3, keepdims=False).astype(jnp.float32)
    tile_k = lax.dynamic_index_in_dim(whole_k, tile, 3, keepdims=False).astype(jnp.float32)
    tile_v = lax.dynamic_index_in_dim(whole_v, tile, 3, keepdims=False).astype(jnp.float32)
    slot_keys = lax.dynamic_index_in_dim(cache_keys, slot, 0, keepdims=False)
    slot_keys = slot_keys.reshape(TPG, N_FSDP, CACHE * TILE, HEADS, HD).astype(jnp.float32)
    slot_values = lax.dynamic_index_in_dim(cache_values, slot, 0, keepdims=False)
    slot_values = slot_values.reshape(TPG, N_FSDP, CACHE * TILE, HEADS, HD).astype(jnp.float32)
    cache_scores = jnp.einsum("bfgihd,bgrhd->bghfir", tile_q, slot_keys) * (HD ** -0.5)
    cache_scores = cache_scores.reshape(TPG, N_FSDP, HEADS, SPAN * TILE, CACHE * TILE)
    span_scores = jnp.einsum("bfgihd,bcgjhd->bghficj", tile_q, tile_k) * (HD ** -0.5)
    span_scores = span_scores.reshape(TPG, N_FSDP, HEADS, SPAN * TILE, SPAN * TILE)
    cache_frame = jnp.arange(CACHE * TILE, dtype=jnp.int32) // TILE
    cache_live = cache_frame[None, None, :] >= (CACHE - cache_frames)[:, :, None]
    span_frame = jnp.arange(SPAN * TILE, dtype=jnp.int32) // TILE
    causal = span_frame[None, :] <= span_frame[:, None]
    scores = jnp.concatenate([
        jnp.where(cache_live[:, :, None, None, :], cache_scores, -jnp.inf),
        jnp.where(causal[None, None, None], span_scores, -jnp.inf)], axis=-1)
    probs = normalized(scores).astype(jnp.float32)
    cache_part = probs[..., :CACHE * TILE].reshape(TPG, N_FSDP, HEADS, SPAN, TILE, CACHE * TILE)
    span_part = probs[..., CACHE * TILE:].reshape(TPG, N_FSDP, HEADS, SPAN, TILE, SPAN, TILE)
    result = jnp.einsum("bghfir,bgrhd->bfgihd", cache_part, slot_values)
    result = result + jnp.einsum("bghficj,bcgjhd->bfgihd", span_part, tile_v)
    return result.astype(jnp.bfloat16)


def reference(queries, key_rows, value_rows, cache_keys, cache_values, cache_frames, neighbors, tile_order, out_weight):
    frame_shape = (TPG * SPAN * N_FSDP, TILES, TILE, HEADS, HD)
    spatial = lax.map(
        lambda trio: spatial_frame(trio[0], trio[1], trio[2], neighbors),
        (queries.reshape(frame_shape), key_rows.reshape(frame_shape), value_rows.reshape(frame_shape)))
    full_shape = (TPG, SPAN, N_FSDP, TILES, TILE, HEADS, HD)
    whole_q = queries.reshape(full_shape)
    whole_k = key_rows.reshape(full_shape)
    whole_v = value_rows.reshape(full_shape)
    slots = jnp.arange(TILES, dtype=jnp.int32)
    temporal = lax.map(
        lambda pair: temporal_slot(pair[0], pair[1], whole_q, whole_k, whole_v, cache_keys, cache_values, cache_frames),
        (slots, tile_order.astype(jnp.int32)))
    inverse = jnp.zeros((TILES,), jnp.int32).at[tile_order].set(slots)
    temporal = jnp.take(temporal, inverse, axis=0)
    temporal = jnp.moveaxis(temporal, 0, 3)
    combined = (spatial.reshape(full_shape).astype(jnp.float32) + temporal.astype(jnp.float32)).astype(jnp.bfloat16)
    combined = combined.reshape(TPG * SPAN, N_FSDP * TOKF, HH)

    def project(row_block):
        return jnp.dot(row_block, out_weight, preferred_element_type=jnp.float32).astype(jnp.bfloat16)

    output = lax.map(project, combined)
    return output.reshape(TPG * SPAN, N_FSDP, TOKF, D)
```

```python
import functools

import jax
import jax.numpy as jnp
from jax import lax
from jax.experimental import pallas as pl
from jax.experimental.pallas import tpu as pltpu
from jax.sharding import PartitionSpec as P

MESH = pl.DeviceIdType.MESH
HEADS = 20
HD = 128
TILE = 8
CACHE = 8
HH = 2560
D = 5120
BF16 = jnp.bfloat16
F32 = jnp.float32
NEG = -1e30
LOG2E = 1.4426950408889634
SCALE2 = HD ** (-0.5) * LOG2E
NT = (((1,), (1,)), ((), ()))


def softmax_parts(scores):
    top = jnp.max(scores, axis=-1, keepdims=True)
    weights = jnp.exp2(scores - top)
    total = jnp.sum(weights, axis=-1, keepdims=True)
    return weights.astype(BF16), 1.0 / total


def kernel(
    q_ref,
    k_ref,
    v_ref,
    perm_ref,
    back_ref,
    near_ref,
    live_ref,
    ck_ref,
    cv_ref,
    w_ref,
    out_ref,
    send,
    recv,
    cache,
    o_send,
    o_recv,
    mixed,
    pair,
    wt,
    out_buf,
    one_s,
    one_r,
    loc,
    qkv_s,
    qkv_r,
    cache_s,
    cache_r,
    o_s,
    o_r,
    z_s,
    z_r,
    y_s,
    y_r,
    x_s,
    x_r,
    m_s,
    m_r,
    out_s,
):
    s = lax.axis_index("seq")
    f = lax.axis_index("fsdp")
    z, y = s // 4, s % 4
    x, c = f // 2, f % 2
    even = (z + 1) % 2
    sigma = 1 - 2 * even
    base = (z // 2) * 2
    me = (z % 2) * 4 + y

    def at(dx=0, dy=0, dz=0):
        return (((z + dz) % 8) * 4 + (y + dy) % 4, ((x + dx) % 4) * 2 + c)

    partner = (s, x * 2 + (1 - c))

    def member(index):
        return ((base + index // 4) * 4 + index % 4, f)

    def remote(src, dst, ss, rs, device):
        return pltpu.make_async_remote_copy(
            src_ref=src, dst_ref=dst, send_sem=ss, recv_sem=rs, device_id=device, device_id_type=MESH
        )

    barrier = pltpu.get_barrier_semaphore()
    greeted = [partner, at(dx=1), at(dx=3)]
    greeted += [member((me + d) % 8) for d in range(1, 8)]
    greeted += [at(dz=sigma), at(dz=2 * sigma + 8), at(dz=3 * sigma + 8)]
    for device in greeted:
        pl.semaphore_signal(barrier, inc=1, device_id=device, device_id_type=MESH)
    pl.semaphore_wait(barrier, len(greeted))

    raw_remote = remote(w_ref, pair.at[pl.ds(c * 320, 320)], one_s.at[0], one_r.at[0], partner)
    raw_remote.start()
    raw_local = pltpu.make_async_copy(w_ref, pair.at[pl.ds(c * 320, 320)], loc.at[0])
    raw_local.start()

    for index, ref in enumerate((q_ref, k_ref, v_ref)):

        @pl.loop(0, 5)
        def _(step, index=index, ref=ref):
            cols = pl.ds(pl.multiple_of(step * 512, 512), 512)
            rows = jnp.dot(perm_ref[...], ref[:, cols], preferred_element_type=F32)
            send[:, index, :, cols] = rows.astype(BF16).reshape(8, 32, 512)

    raw_local.wait()
    raw_remote.wait()
    pick = lax.broadcasted_iota(jnp.int32, (80, 160), 1) == (
        lax.broadcasted_iota(jnp.int32, (80, 160), 0) + c * 80
    )
    chunk = lax.dot_general(
        jnp.where(pick, 1.0, 0.0).astype(BF16), pair[...], NT, preferred_element_type=F32
    )
    half = pl.ds(pl.multiple_of(c * 80, 16), 80)

    def lanes(dx):
        return pl.ds(pl.multiple_of(((x + dx) % 4) * 640, 128), 640)

    wt[z, y, half, lanes(0)] = chunk.astype(BF16)

    def zof(i):
        rel = -((i + 1) // 2) if i % 2 else i // 2
        return (z + rel + 8) % 8

    def z_move(i, step):
        ref = wt.at[zof(i), y, half, lanes(0)]
        to_right = step[0] == "r"
        slot = step[1] + (0 if to_right else 4)
        return remote(ref, ref, z_s.at[slot], z_r.at[slot], at(dz=1 if to_right else 7))

    def y_move(i, kind):
        if kind == 0:
            ref, device = wt.at[zof(i), y, half, lanes(0)], at(dy=1)
        elif kind == 1:
            ref, device = wt.at[zof(i), y, half, lanes(0)], at(dy=3)
        elif i % 2 == 0:
            ref, device = wt.at[zof(i), (y + 3) % 4, half, lanes(0)], at(dy=1)
        else:
            ref, device = wt.at[zof(i), (y + 1) % 4, half, lanes(0)], at(dy=3)
        return remote(ref, ref, y_s.at[i, kind], y_r.at[i, kind], device)

    def x_move(i, kind):
        if kind == 0:
            ref, device = wt.at[zof(i), :, half, lanes(0)], at(dx=1)
        elif kind == 1:
            ref, device = wt.at[zof(i), :, half, lanes(0)], at(dx=3)
        elif kind == 2:
            ref, device = wt.at[zof(i), pl.ds(0, 2), half, lanes(3)], at(dx=1)
        else:
            ref, device = wt.at[zof(i), pl.ds(2, 2), half, lanes(1)], at(dx=3)
        return remote(ref, ref, x_s.at[i, kind], x_r.at[i, kind], device)

    def mirror(i):
        ref = wt.at[zof(i), :, half]
        return remote(ref, ref, m_s.at[i], m_r.at[i], partner)

    z_move(0, ("r", 0)).start()
    z_move(0, ("l", 0)).start()
    y_move(0, 0).start()
    y_move(0, 1).start()

    qkv_moves = []
    for d in range(1, 8):
        to = (me + d) % 8
        qkv_moves.append(
            remote(send.at[to], recv.at[me], qkv_s.at[d], qkv_r.at[d], member(to))
        )
    cache_moves = []
    for j, off in ((1, sigma), (2, 8 - 2 * sigma), (3, 3 * sigma + 8)):
        to_z = (z + off + 8) % 8
        for n, ref in enumerate((ck_ref, cv_ref)):
            cache_moves.append(
                remote(
                    ref.at[to_z // 2], cache.at[j, n], cache_s.at[j, n], cache_r.at[j, n], (to_z * 4 + y, f)
                )
            )
    for move in qkv_moves + cache_moves:
        move.start()
    locals_ = [
        pltpu.make_async_copy(send.at[me], recv.at[me], loc.at[1]),
        pltpu.make_async_copy(ck_ref.at[z // 2], cache.at[0, 0], loc.at[2]),
        pltpu.make_async_copy(cv_ref.at[z // 2], cache.at[0, 1], loc.at[3]),
    ]
    for move in locals_:
        move.start()

    def spatial(first, count):
        @pl.loop(first, first + count)
        def _(h):
            cols = pl.ds(pl.multiple_of(h * HD, HD), HD)
            scores = lax.dot_general(q_ref[:, cols], k_ref[:, cols], NT, preferred_element_type=F32)
            weights, inverse = softmax_parts(scores * SCALE2 + near_ref[...])
            values = jnp.dot(weights, v_ref[:, cols], preferred_element_type=F32)
            mixed[:, cols] = (values * inverse).astype(BF16)

    for i in range(1, 8):
        k = (i + 1) // 2
        if i % 2:
            z_move(i, ("r", k - 1)).wait_recv()
            if k < 4:
                z_move(i, ("r", k)).start()
        else:
            z_move(i, ("l", k - 1)).wait_recv()
            if k < 3:
                z_move(i, ("l", k)).start()
        y_move(i, 0).start()
        y_move(i, 1).start()

    def y_steps(i):
        y_move(i, 0).wait_recv()
        if i % 2 == 0:
            y_move(i, 2).start()
        y_move(i, 1).wait_recv()
        if i % 2:
            y_move(i, 2).start()
        y_move(i, 2).wait_recv()
        x_move(i, 0).start()
        x_move(i, 1).start()

    def x_steps(i):
        x_move(i, 0).wait_recv()
        x_move(i, 2).start()
        x_move(i, 1).wait_recv()
        x_move(i, 3).start()

    def x_last(i):
        x_move(i, 2).wait_recv()
        x_move(i, 3).wait_recv()
        mirror(i).start()

    for i in range(8):
        y_steps(i)
        if i > 0:
            x_steps(i - 1)
        if i > 1:
            x_last(i - 2)
        if i < 5:
            spatial(i * 4, 4)

    for move in locals_:
        move.wait()
    for move in qkv_moves + cache_moves:
        move.wait_recv()

    for p in range(2):

        @pl.loop(0, HEADS)
        def _(h, p=p):
            cols = pl.ds(pl.multiple_of(h * HD, HD), HD)
            rows = pl.ds(p * 16, 16)
            slots = pl.ds(p * 2, 2)
            queries = recv[:, 0, rows, cols].reshape(128, HD)
            span_k = recv[:, 1, rows, cols].reshape(128, HD)
            span_v = recv[:, 2, rows, cols].reshape(128, HD)
            old_k = cache[slots, 0, :, cols].reshape(128, HD)
            old_v = cache[slots, 1, :, cols].reshape(128, HD)
            keys = jnp.concatenate([span_k, old_k], axis=0)
            values = jnp.concatenate([span_v, old_v], axis=0)
            scores = lax.dot_general(queries, keys, NT, preferred_element_type=F32)
            weights, inverse = softmax_parts(scores * SCALE2 + live_ref[...])
            result = jnp.dot(weights, values, preferred_element_type=F32) * inverse
            o_send[:, rows, cols] = result.astype(BF16).reshape(8, 16, HD)

    o_moves = []
    for d in range(1, 8):
        to = (me + d) % 8
        o_moves.append(remote(o_send.at[to], o_recv.at[me], o_s.at[d], o_r.at[d], member(to)))
    for move in o_moves:
        move.start()
    o_local = pltpu.make_async_copy(o_send.at[me], o_recv.at[me], loc.at[4])
    o_local.start()

    x_steps(7)
    x_last(6)

    o_local.wait()
    for move in o_moves:
        move.wait_recv()

    @pl.loop(0, 5)
    def _(step):
        cols = pl.ds(pl.multiple_of(step * 512, 512), 512)
        rows = jnp.dot(back_ref[...], o_recv[:, :, cols].reshape(256, 512), preferred_element_type=F32)
        mixed[:, cols] = (mixed[:, cols].astype(F32) + rows).astype(BF16)

    def out_move(i):
        cols = pl.ds(pl.multiple_of(zof(i) * 640, 128), 640)
        return pltpu.make_async_copy(out_buf.at[i % 2], out_ref.at[:, cols], out_s.at[i % 2])

    def project(i):
        mirror(i).wait_recv()
        if i > 1:
            out_move(i - 2).wait()
        block = wt[zof(i)].reshape(640, HH)
        result = lax.dot_general(mixed[...], block, NT, preferred_element_type=F32)
        out_buf[i % 2] = result.astype(BF16)
        out_move(i).start()

    for i in range(7):
        project(i)
    x_last(7)
    project(7)
    out_move(6).wait()
    out_move(7).wait()

    for move in qkv_moves + cache_moves + o_moves:
        move.wait_send()
    for k in range(4):
        z_move(0, ("r", k)).wait_send()
    for k in range(3):
        z_move(0, ("l", k)).wait_send()
    for i in range(8):
        for kind in range(3):
            y_move(i, kind).wait_send()
        for kind in range(4):
            x_move(i, kind).wait_send()
        mirror(i).wait_send()


def shards(queries, key_rows, value_rows, cache_keys, cache_values, cache_frames, neighbors, tile_order, out_weight):
    s = lax.axis_index("seq")
    block = s // 8
    tokens = jnp.arange(256, dtype=jnp.int32)
    index, j, tok = tokens // 32, (tokens // 8) % 4, tokens % 8
    side = index // 4
    slot = ((block * 2 + side + j * (2 * side - 1) + 8) % 8) * 4 + index % 4
    tile_ids = jnp.arange(32, dtype=jnp.int32)
    tile = jnp.sum(jnp.where(slot[:, None] == tile_ids[None, :], tile_order[None, :], 0), axis=1)
    source = tile * 8 + tok
    perm = (source[:, None] == tokens[None, :]).astype(BF16)
    back = (tokens[:, None] == source[None, :]).astype(BF16)
    near = jnp.any(neighbors[:, :, None] == tile_ids[None, None, :], axis=1)
    near = jnp.where(near, 0.0, NEG).astype(F32)
    near = jnp.broadcast_to(near[:, None, :, None], (32, 8, 32, 8)).reshape(256, 256)
    rows = jnp.arange(128, dtype=jnp.int32)
    row_frame, row_slot = rows // 16, (rows // 8) % 2
    span = (row_slot[:, None] == row_slot[None, :]) & (row_frame[None, :] <= row_frame[:, None])
    frames = jnp.sum(jnp.where(jnp.arange(4, dtype=jnp.int32) == block, cache_frames[:, 0], 0))
    old = (row_slot[:, None] == rows[None, :] // 64) & ((rows[None, :] // 8) % 8 >= CACHE - frames)
    live = jnp.where(jnp.concatenate([span, old], axis=1), 0.0, NEG).astype(F32)

    vmem = pl.BlockSpec(memory_space=pltpu.VMEM)
    hbm = pl.BlockSpec(memory_space=pl.ANY)
    dma = pltpu.SemaphoreType.DMA
    out = pl.pallas_call(
        kernel,
        out_shape=jax.ShapeDtypeStruct((256, D), BF16),
        in_specs=[vmem] * 7 + [hbm] * 3,
        out_specs=hbm,
        scratch_shapes=[
            pltpu.VMEM((8, 3, 32, HH), BF16),
            pltpu.VMEM((8, 3, 32, HH), BF16),
            pltpu.VMEM((4, 2, 64, HH), BF16),
            pltpu.VMEM((8, 32, HH), BF16),
            pltpu.VMEM((8, 32, HH), BF16),
            pltpu.VMEM((256, HH), BF16),
            pltpu.VMEM((640, 160), BF16),
            pltpu.VMEM((8, 4, 160, HH), BF16),
            pltpu.VMEM((2, 256, 640), BF16),
            dma((1,)),
            dma((1,)),
            dma((5,)),
            dma((8,)),
            dma((8,)),
            dma((4, 2)),
            dma((4, 2)),
            dma((8,)),
            dma((8,)),
            dma((8,)),
            dma((8,)),
            dma((8, 3)),
            dma((8, 3)),
            dma((8, 4)),
            dma((8, 4)),
            dma((8,)),
            dma((8,)),
            dma((2,)),
        ],
        compiler_params=pltpu.CompilerParams(
            collective_id=0, has_side_effects=True, vmem_limit_bytes=60 * 2**20
        ),
        cost_estimate=pl.CostEstimate(flops=9 * 10**9, bytes_accessed=2 * 10**7, transcendentals=3 * 10**6),
    )(
        queries.reshape(256, HH),
        key_rows.reshape(256, HH),
        value_rows.reshape(256, HH),
        perm,
        back,
        near,
        live,
        cache_keys.reshape(4, 64, HH),
        cache_values.reshape(4, 64, HH),
        out_weight,
    )
    return out.reshape(1, 1, 256, D)


def solution(mesh):
    placed = (
        P("seq", "fsdp", None, None),
        P("seq", "fsdp", None, None),
        P("seq", "fsdp", None, None),
        P("seq", None, "fsdp", None, None),
        P("seq", None, "fsdp", None, None),
        P(None, "fsdp"),
        P(),
        P(),
        P("fsdp", "seq"),
    )
    return jax.shard_map(
        shards, mesh=mesh, in_specs=placed, out_specs=P("seq", "fsdp", None, None), check_vma=False
    )
```

```python
import functools

import jax
import jax.numpy as jnp
from jax import lax
from jax.experimental import pallas as pl
from jax.experimental.pallas import tpu as pltpu
from jax.sharding import PartitionSpec as P

MESH = pl.DeviceIdType.MESH
HEADS = 20
HD = 128
TILE = 8
CACHE = 8
HH = 2560
HALF = 1280
TEMPORAL_UNROLL = 5
SCHEDULE = ('k1', 'z1', 'z2', 'y0', 'z3', 'z4', 'y1', 'z5', 'z6', 'y2', 'z7', 'a0', 'a1', 's0', 'x0', 'l0', 'y3', 's1', 'x1', 'l1', 'y4', 's2', 'y5', 's3', 'x2', 'l2', 's4', 'y6', 'y7', 't0', 'x3', 'l3', 'x4', 'l4', 'c0', 'p0', 'p1', 'p2', 'p3', 'x5', 'l5', 'p4', 't1', 'x6', 'l6', 'p5', 'c1', 'p10', 'p11', 'p12', 'x7', 'p13', 'p14', 'p15', 'p6', 'p16', 'l7', 'p7', 'p17')
D = 5120
BF16 = jnp.bfloat16
F32 = jnp.float32
NEG = -1e30
LOG2E = 1.4426950408889634
SCALE2 = HD ** (-0.5) * LOG2E
NT = (((1,), (1,)), ((), ()))


def softmax_parts(scores):
    top = jnp.max(scores, axis=-1, keepdims=True)
    weights = jnp.exp2(scores - top)
    total = jnp.sum(weights, axis=-1, keepdims=True)
    return weights.astype(BF16), 1.0 / total


def tables(z, order_ref, near_tiles_ref, frames_ref, perm_ref, back_ref, near_ref, live_ref):
    def iota(shape, dim):
        return lax.broadcasted_iota(jnp.int32, shape, dim)

    def slot_of(token):
        index, j = token // 32, (token // 8) % 4
        side = index // 4
        return (((z // 2) * 2 + side + j * (2 * side - 1) + 8) % 8) * 4 + index % 4

    order = order_ref[...]
    held = iota((256, 32), 1) == slot_of(iota((256, 32), 0))
    tile = jnp.sum(jnp.where(held, jnp.broadcast_to(order, (256, 32)), 0), axis=1, keepdims=True)
    source = tile * 8 + iota((256, 1), 0) % 8
    perm_ref[...] = jnp.where(source == iota((256, 256), 1), 1.0, 0.0).astype(BF16)
    held = iota((32, 256), 0) == slot_of(iota((32, 256), 1))
    tile = jnp.dot(
        jnp.broadcast_to(order, (8, 32)).astype(F32).astype(BF16),
        jnp.where(held, 1.0, 0.0).astype(BF16),
        preferred_element_type=F32,
    )[:1].astype(jnp.int32)
    source = tile * 8 + iota((1, 256), 1) % 8
    back_ref[...] = jnp.where(source == iota((256, 256), 0), 1.0, 0.0).astype(BF16)

    mine = iota((256, 32), 1) == iota((256, 32), 0) // 8
    tiles = lax.dot_general(
        jnp.where(mine, 1.0, 0.0).astype(BF16),
        near_tiles_ref[...].astype(F32).astype(BF16),
        NT,
        preferred_element_type=F32,
    ).astype(jnp.int32)
    column = iota((256, 256), 1) // 8
    near = tiles[:, 0:1] == column
    for n in range(1, 9):
        near = near | (tiles[:, n : n + 1] == column)
    near_ref[...] = jnp.where(near, 0.0, NEG)

    row, col = iota((128, 256), 0), iota((128, 256), 1)
    span = (col < 128) & ((row // 8) % 2 == (col // 8) % 2) & (col // 16 <= row // 16)
    old = (col >= 128) & ((row // 8) % 2 == (col - 128) // 64)
    old = old & ((col // 8) % 8 >= CACHE - frames_ref[0, z // 2])
    live_ref[...] = jnp.where(span | old, 0.0, NEG)


def kernel(
    q_hbm,
    k_hbm,
    v_hbm,
    order_ref,
    near_tiles_ref,
    frames_ref,
    ck_ref,
    cv_ref,
    w_ref,
    out_ref,
    send,
    recv,
    cache,
    o_send,
    o_recv,
    mixed,
    q_ref,
    k_ref,
    v_ref,
    perm_ref,
    back_ref,
    near_ref,
    live_ref,
    pair,
    wt,
    out_buf,
    total,
    one_s,
    one_r,
    loc,
    qkv_s,
    qkv_r,
    cache_s,
    cache_r,
    o_s,
    o_r,
    z_s,
    z_r,
    y_s,
    y_r,
    x_s,
    x_r,
    f_s,
    f_r,
    m_s,
    m_r,
    out_s,
):
    s = lax.axis_index("seq")
    f = lax.axis_index("fsdp")
    z, y = s // 4, s % 4
    x, c = f // 2, f % 2
    even = (z + 1) % 2
    sigma = 1 - 2 * even
    base = (z // 2) * 2
    me = (z % 2) * 4 + y

    def at(dx=0, dy=0, dz=0):
        return (((z + dz) % 8) * 4 + (y + dy) % 4, ((x + dx) % 4) * 2 + c)

    partner = (s, x * 2 + (1 - c))

    def member(index):
        return ((base + index // 4) * 4 + index % 4, f)

    def remote(src, dst, ss, rs, device):
        return pltpu.make_async_remote_copy(
            src_ref=src, dst_ref=dst, send_sem=ss, recv_sem=rs, device_id=device, device_id_type=MESH
        )

    half = pl.ds(pl.multiple_of(c * 80, 16), 80)
    barrier = pltpu.get_barrier_semaphore()
    greeted = [partner, at(dx=1), at(dx=3)]
    greeted += [member((me + d) % 8) for d in range(1, 8)]
    greeted += [at(dz=sigma), at(dz=2 * sigma + 8), at(dz=3 * sigma + 8)]
    for device in greeted:
        pl.semaphore_signal(barrier, inc=1, device_id=device, device_id_type=MESH)
    staged = [
        pltpu.make_async_copy(src, dst, loc.at[1, n])
        for n, (src, dst) in enumerate(((q_hbm, q_ref), (k_hbm, k_ref), (v_hbm, v_ref)))
    ]
    for move in staged:
        move.start()
    raw_local = pltpu.make_async_copy(w_ref.at[half], pair.at[c], loc.at[0, 0])
    raw_local.start()
    pl.semaphore_wait(barrier, len(greeted))

    other = pl.ds(pl.multiple_of((1 - c) * 80, 16), 80)
    raw_remote = remote(w_ref.at[other], pair.at[c], one_s.at[0], one_r.at[0], partner)
    raw_remote.start()
    def pack(h):
        for index, ref in enumerate((q_ref, k_ref, v_ref)):

            @pl.loop(0, 5)
            def _(step, index=index, ref=ref):
                cols = pl.ds(pl.multiple_of(step * 256, 256), 256)
                from_cols = pl.ds(pl.multiple_of(h * HALF + step * 256, 256), 256)
                rows = jnp.dot(perm_ref[...], ref[:, from_cols], preferred_element_type=F32)
                send[h, :, index, :, cols] = rows.astype(BF16).reshape(8, 32, 256)

    raw_local.wait()
    raw_remote.wait()
    chunk = jnp.concatenate([pair[0].astype(F32), pair[1].astype(F32)], axis=1)

    def lanes(dx):
        return pl.ds(pl.multiple_of(((x + dx) % 4) * 640, 128), 640)

    wt[z, y, half, lanes(0)] = chunk.astype(BF16)

    def zof(i):
        rel = -((i + 1) // 2) if i % 2 else i // 2
        return (z + rel + 8) % 8

    def z_move(i, step):
        ref = wt.at[zof(i), y, half, lanes(0)]
        to_right = step[0] == "r"
        slot = step[1] + (0 if to_right else 4)
        return remote(ref, ref, z_s.at[slot], z_r.at[slot], at(dz=1 if to_right else 7))

    def y_move(i, kind):
        if kind == 0:
            ref, device = wt.at[zof(i), y, half, lanes(0)], at(dy=1)
        elif kind == 1:
            ref, device = wt.at[zof(i), y, half, lanes(0)], at(dy=3)
        else:
            ref, device = wt.at[zof(i), y, half, lanes(0)], at(dy=2)
        return remote(ref, ref, y_s.at[i, kind], y_r.at[i, kind], device)

    def x_move(i, kind):
        if kind == 0:
            ref, device = wt.at[zof(i), :, half, lanes(0)], at(dx=1)
        elif kind == 1:
            ref, device = wt.at[zof(i), :, half, lanes(0)], at(dx=3)
        elif kind == 2:
            ref, device = wt.at[zof(i), pl.ds(0, 2), half, lanes(3)], at(dx=1)
        else:
            ref, device = wt.at[zof(i), pl.ds(2, 2), half, lanes(1)], at(dx=3)
        return remote(ref, ref, x_s.at[i, kind], x_r.at[i, kind], device)

    def x_first(r, kind):
        row = (y + r) % 4
        if kind < 2:
            ref, device = wt.at[z, row, half, lanes(0)], at(dx=3 if kind else 1)
        elif r < 2:
            ref, device = wt.at[z, row, half, lanes(3)], at(dx=1)
        else:
            ref, device = wt.at[z, row, half, lanes(1)], at(dx=3)
        return remote(ref, ref, f_s.at[r, kind], f_r.at[r, kind], device)

    def last_mirror(n):
        rows = pl.ds(0, 2) if n == 3 else pl.ds(2, 2) if n == 4 else pl.ds(0, 4)
        ref = wt.at[zof(7), rows, half, lanes((0, 3, 1, 2, 2)[n])]
        return remote(ref, ref, m_s.at[7 + n], m_r.at[7 + n], partner)

    def mirror(i):
        ref = wt.at[zof(i), :, half]
        return remote(ref, ref, m_s.at[i], m_r.at[i], partner)

    x_first(0, 0).start()
    x_first(0, 1).start()
    z_move(0, ("r", 0)).start()
    z_move(0, ("l", 0)).start()
    for kind in range(3):
        y_move(0, kind).start()
    for move in staged:
        move.wait()
    tables(z, order_ref, near_tiles_ref, frames_ref, perm_ref, back_ref, near_ref, live_ref)
    pack(0)

    def exchange(h):
        moves = []
        lane_half = pl.ds(h * HALF, HALF)
        for j, off in ((1, sigma), (2, 8 - 2 * sigma), (3, 3 * sigma + 8)):
            to_z = (z + off + 8) % 8
            for n, ref in enumerate((ck_ref, cv_ref)):
                src = ref.at[to_z // 2, :, lane_half]
                sems = cache_s.at[h, j, n], cache_r.at[h, j, n]
                moves.append(remote(src, cache.at[h, j, n], *sems, (to_z * 4 + y, f)))
        for d in range(1, 8):
            to = (me + d) % 8
            sems = qkv_s.at[h, d], qkv_r.at[h, d]
            moves.append(remote(send.at[h, to], recv.at[h, me], *sems, member(to)))
        own = [pltpu.make_async_copy(send.at[h, me], recv.at[h, me], loc.at[h, 1])]
        for n, ref in enumerate((ck_ref, cv_ref)):
            src = ref.at[z // 2, :, lane_half]
            own.append(pltpu.make_async_copy(src, cache.at[h, 0, n], loc.at[h, 2 + n]))
        return moves, own

    exchanges = [exchange(0), exchange(1)]

    def start_exchange(h):
        for move in exchanges[h][0] + exchanges[h][1]:
            move.start()

    def spatial(first, count):
        @pl.loop(first, first + count)
        def _(h):
            cols = pl.ds(pl.multiple_of(h * HD, HD), HD)
            scores = lax.dot_general(q_ref[:, cols], k_ref[:, cols], NT, preferred_element_type=F32)
            weights, inverse = softmax_parts(scores * SCALE2 + near_ref[...])
            values = jnp.dot(weights, v_ref[:, cols], preferred_element_type=F32)
            mixed[:, cols] = (values * inverse).astype(BF16)

    def z_steps(i):
        k = (i + 1) // 2
        if i % 2:
            z_move(i, ("r", k - 1)).wait_recv()
            if k < 4:
                z_move(i, ("r", k)).start()
        else:
            z_move(i, ("l", k - 1)).wait_recv()
            if k < 3:
                z_move(i, ("l", k)).start()
        y_move(i, 0).start()
        y_move(i, 1).start()
        y_move(i, 2).start()

    def y_steps(i):
        for kind, r in enumerate((3, 1, 2)):
            y_move(i, kind).wait_recv()
            if i == 0:
                x_first(r, 0).start()
                x_first(r, 1).start()
        if i:
            x_move(i, 0).start()
            x_move(i, 1).start()

    def x_steps(i):
        if i == 0:
            for r in (0, 3, 1, 2):
                x_first(r, 0).wait_recv()
                if r < 2:
                    x_first(r, 2).start()
                x_first(r, 1).wait_recv()
                if r >= 2:
                    x_first(r, 2).start()
            return
        x_move(i, 0).wait_recv()
        x_move(i, 2).start()
        if i == 7:
            last_mirror(1).start()
        x_move(i, 1).wait_recv()
        x_move(i, 3).start()
        if i == 7:
            last_mirror(2).start()

    def x_last(i):
        if i == 0:
            for r in range(4):
                x_first(r, 2).wait_recv()
        elif i == 7:
            last_mirror(0).start()
            x_move(i, 2).wait_recv()
            last_mirror(3).start()
            x_move(i, 3).wait_recv()
            last_mirror(4).start()
            return
        else:
            x_move(i, 2).wait_recv()
            x_move(i, 3).wait_recv()
        mirror(i).start()

    def o_exchange(h):
        moves = []
        for d in range(1, 8):
            to = (me + d) % 8
            sems = o_s.at[h, d], o_r.at[h, d]
            moves.append(remote(o_send.at[h, to], o_recv.at[h, me], *sems, member(to)))
        return moves, pltpu.make_async_copy(o_send.at[h, me], o_recv.at[h, me], loc.at[h, 4])

    o_exchanges = [o_exchange(0), o_exchange(1)]

    def temporal(h):
        moves, own = exchanges[h]
        for move in own:
            move.wait()
        for move in moves:
            move.wait_recv()

        for p in range(2):
            rows = pl.ds(p * 16, 16)
            slots = pl.ds(p * 2, 2)

            def head(cols):
                queries = recv[h, :, 0, rows, cols].reshape(128, HD)
                span_k = recv[h, :, 1, rows, cols].reshape(128, HD)
                span_v = recv[h, :, 2, rows, cols].reshape(128, HD)
                old_k = cache[h, slots, 0, :, cols].reshape(128, HD)
                old_v = cache[h, slots, 1, :, cols].reshape(128, HD)
                keys = jnp.concatenate([span_k, old_k], axis=0)
                values = jnp.concatenate([span_v, old_v], axis=0)
                scores = lax.dot_general(queries, keys, NT, preferred_element_type=F32)
                weights, inverse = softmax_parts(scores * SCALE2 + live_ref[...])
                result = jnp.dot(weights, values, preferred_element_type=F32) * inverse
                o_send[h, :, rows, cols] = result.astype(BF16).reshape(8, 16, HD)

            @pl.loop(0, 10 // TEMPORAL_UNROLL)
            def _(step, head=head):
                for n in range(TEMPORAL_UNROLL):
                    head(pl.ds(pl.multiple_of((step * TEMPORAL_UNROLL + n) * HD, HD), HD))

        moves, own = o_exchanges[h]
        for move in moves:
            move.start()
        own.start()

    def combine(h):
        moves, own = o_exchanges[h]
        own.wait()
        for move in moves:
            move.wait_recv()

        @pl.loop(0, 5)
        def _(step):
            cols = pl.ds(pl.multiple_of(step * 256, 256), 256)
            to_cols = pl.ds(pl.multiple_of(h * HALF + step * 256, 256), 256)
            rows = jnp.dot(
                back_ref[...], o_recv[h, :, :, cols].reshape(256, 256), preferred_element_type=F32
            )
            mixed[:, to_cols] = (mixed[:, to_cols].astype(F32) + rows).astype(BF16)

    def out_move(i):
        cols = pl.ds(pl.multiple_of(zof(i) * 640, 128), 640)
        return pltpu.make_async_copy(out_buf.at[i % 2], out_ref.at[:, cols], out_s.at[i % 2])

    def project(i, h):
        lane_half = pl.ds(h * HALF, HALF)
        if h == 0 and i < 7:
            mirror(i).wait_recv()
        elif h == 0:
            for n in range(5):
                last_mirror(n).wait_recv()
        block = wt[zof(i), :, :, lane_half].reshape(640, HALF)
        result = lax.dot_general(mixed[:, lane_half], block, NT, preferred_element_type=F32)
        if h == 0:
            total[i] = result
        else:
            if i > 1:
                out_move(i - 2).wait()
            out_buf[i % 2] = (result + total[i]).astype(BF16)
            out_move(i).start()

    def run(step):
        kind, index = step[0], int(step[1:])
        if kind == "z":
            z_steps(index)
        elif kind == "y":
            y_steps(index)
        elif kind == "x":
            x_steps(index)
        elif kind == "l":
            x_last(index)
        elif kind == "s":
            spatial(index * 4, 4)
        elif kind == "k":
            pack(index)
        elif kind == "a":
            start_exchange(index)
        elif kind == "t":
            temporal(index)
        elif kind == "c":
            combine(index)
        elif kind == "p":
            project(index % 10, index // 10)

    for step in SCHEDULE:
        run(step)
    out_move(6).wait()
    out_move(7).wait()

    for h in range(2):
        for move in exchanges[h][0] + o_exchanges[h][0]:
            move.wait_send()
    for k in range(4):
        z_move(0, ("r", k)).wait_send()
    for k in range(3):
        z_move(0, ("l", k)).wait_send()
    for i in range(8):
        for kind in range(3):
            y_move(i, kind).wait_send()
        for kind in range(4 if i else 0):
            x_move(i, kind).wait_send()
        if i < 7:
            mirror(i).wait_send()
    for r in range(4):
        for kind in range(3):
            x_first(r, kind).wait_send()
    for n in range(5):
        last_mirror(n).wait_send()


def shards(queries, key_rows, value_rows, cache_keys, cache_values, cache_frames, neighbors, tile_order, out_weight):
    vmem = pl.BlockSpec(memory_space=pltpu.VMEM)
    hbm = pl.BlockSpec(memory_space=pl.ANY)
    dma = pltpu.SemaphoreType.DMA
    out = pl.pallas_call(
        kernel,
        out_shape=jax.ShapeDtypeStruct((256, D), BF16),
        in_specs=[hbm] * 3 + [vmem] * 2 + [pl.BlockSpec(memory_space=pltpu.SMEM)] + [hbm] * 3,
        out_specs=hbm,
        scratch_shapes=[
            pltpu.VMEM((2, 8, 3, 32, HALF), BF16),
            pltpu.VMEM((2, 8, 3, 32, HALF), BF16),
            pltpu.VMEM((2, 4, 2, 64, HALF), BF16),
            pltpu.VMEM((2, 8, 32, HALF), BF16),
            pltpu.VMEM((2, 8, 32, HALF), BF16),
            pltpu.VMEM((256, HH), BF16),
            pltpu.VMEM((256, HH), BF16),
            pltpu.VMEM((256, HH), BF16),
            pltpu.VMEM((256, HH), BF16),
            pltpu.VMEM((256, 256), BF16),
            pltpu.VMEM((256, 256), BF16),
            pltpu.VMEM((256, 256), F32),
            pltpu.VMEM((128, 256), F32),
            pltpu.VMEM((2, 80, 320), BF16),
            pltpu.VMEM((8, 4, 160, HH), BF16),
            pltpu.VMEM((2, 256, 640), BF16),
            pltpu.VMEM((8, 256, 640), F32),
            dma((1,)),
            dma((1,)),
            dma((2, 5)),
            dma((2, 8)),
            dma((2, 8)),
            dma((2, 4, 2)),
            dma((2, 4, 2)),
            dma((2, 8)),
            dma((2, 8)),
            dma((8,)),
            dma((8,)),
            dma((8, 3)),
            dma((8, 3)),
            dma((8, 4)),
            dma((8, 4)),
            dma((4, 3)),
            dma((4, 3)),
            dma((12,)),
            dma((12,)),
            dma((2,)),
        ],
        compiler_params=pltpu.CompilerParams(
            collective_id=0, has_side_effects=True, vmem_limit_bytes=60 * 2**20
        ),
        cost_estimate=pl.CostEstimate(flops=9 * 10**9, bytes_accessed=2 * 10**7, transcendentals=3 * 10**6),
    )(
        queries.reshape(256, HH),
        key_rows.reshape(256, HH),
        value_rows.reshape(256, HH),
        tile_order.reshape(1, 32),
        neighbors.T,
        cache_frames.T,
        cache_keys.reshape(4, 64, HH),
        cache_values.reshape(4, 64, HH),
        out_weight.T,
    )
    return out.reshape(1, 1, 256, D)


def solution(mesh):
    placed = (
        P("seq", "fsdp", None, None),
        P("seq", "fsdp", None, None),
        P("seq", "fsdp", None, None),
        P("seq", None, "fsdp", None, None),
        P("seq", None, "fsdp", None, None),
        P(None, "fsdp"),
        P(),
        P(),
        P("fsdp", "seq"),
    )
    return jax.shard_map(
        shards, mesh=mesh, in_specs=placed, out_specs=P("seq", "fsdp", None, None), check_vma=False
    )
```

```python
import functools

import jax
import jax.numpy as jnp
from jax import lax
from jax.experimental import pallas as pl
from jax.experimental.pallas import tpu as pltpu
from jax.sharding import PartitionSpec as P

MESH = pl.DeviceIdType.MESH
HEADS = 20
HD = 128
TILE = 8
CACHE = 8
HH = 2560
HALF = 1280
TEMPORAL_UNROLL = 5
SCHEDULE = ('z1', 'z2', 'y0', 'b0', 'z3', 'z4', 'y1', 'k0', 'z5', 'z6', 'y2', 'z7', 'a0', 'x0', 'k1', 's0', 'y3', 's1', 'y4', 's2', 'y5', 's3', 'y6', 's4', 'y7', 'a1', 't0', 'x1', 'x2', 'x3', 'x4', 'x5', 'x6', 'x7', 'l0', 'l1', 'l2', 'l3', 'l4', 'l5', 't1', 'l6', 'c0', 'p0', 'p1', 'p2', 'p3', 'p4', 'p5', 'p6', 'c1', 'p10', 'p11', 'p12', 'p13', 'p14', 'p15', 'p16', 'l7', 'p7', 'p17')
D = 5120
BF16 = jnp.bfloat16
F32 = jnp.float32
NEG = -1e30
LOG2E = 1.4426950408889634
SCALE2 = HD ** (-0.5) * LOG2E
NT = (((1,), (1,)), ((), ()))


def softmax_parts(scores):
    top = jnp.max(scores, axis=-1, keepdims=True)
    weights = jnp.exp2(scores - top)
    total = jnp.sum(weights, axis=-1, keepdims=True)
    return weights.astype(BF16), 1.0 / total


def tables(z, order_ref, near_tiles_ref, frames_ref, perm_ref, back_ref, near_ref, live_ref):
    def iota(shape, dim):
        return lax.broadcasted_iota(jnp.int32, shape, dim)

    def slot_of(token):
        index, j = token >> 5, (token >> 3) & 3
        side = index >> 2
        return ((((z // 2) * 2 + side + j * (2 * side - 1) + 8) & 7) << 2) + (index & 3)

    order = order_ref[...]
    held = iota((256, 32), 1) == slot_of(iota((256, 32), 0))
    tile = jnp.sum(jnp.where(held, jnp.broadcast_to(order, (256, 32)), 0), axis=1, keepdims=True)
    source = tile * 8 + (iota((256, 1), 0) & 7)
    perm_ref[...] = jnp.where(source == iota((256, 256), 1), 1.0, 0.0).astype(BF16)
    held = iota((32, 256), 0) == slot_of(iota((32, 256), 1))
    tile = jnp.dot(
        jnp.broadcast_to(order, (8, 32)).astype(F32).astype(BF16),
        jnp.where(held, 1.0, 0.0).astype(BF16),
        preferred_element_type=F32,
    )[:1].astype(jnp.int32)
    source = tile * 8 + (iota((1, 256), 1) & 7)
    back_ref[...] = jnp.where(source == iota((256, 256), 0), 1.0, 0.0).astype(BF16)

    mine = iota((256, 32), 1) == iota((256, 32), 0) >> 3
    tiles = lax.dot_general(
        jnp.where(mine, 1.0, 0.0).astype(BF16),
        near_tiles_ref[...].astype(F32).astype(BF16),
        NT,
        preferred_element_type=F32,
    ).astype(jnp.int32)
    column = iota((256, 256), 1) >> 3
    near = tiles[:, 0:1] == column
    for n in range(1, 9):
        near = near | (tiles[:, n : n + 1] == column)
    near_ref[...] = jnp.where(near, 0.0, NEG)

    row, col = iota((128, 256), 0), iota((128, 256), 1)
    side = (row >> 3) & 1
    span = (col < 128) & (side == (col >> 3) & 1) & (col >> 4 <= row >> 4)
    old = (col >= 128) & (side == (col >> 6) & 1)
    old = old & ((col >> 3) & 7 >= CACHE - frames_ref[0, z // 2])
    live_ref[...] = jnp.where(span | old, 0.0, NEG)


def kernel(
    q_hbm,
    k_hbm,
    v_hbm,
    order_ref,
    near_tiles_ref,
    frames_ref,
    ck_ref,
    cv_ref,
    w_ref,
    out_ref,
    send,
    recv,
    cache,
    o_send,
    o_recv,
    mixed,
    q_ref,
    k_ref,
    v_ref,
    perm_ref,
    back_ref,
    near_ref,
    live_ref,
    pair,
    wt,
    out_buf,
    total,
    one_s,
    one_r,
    loc,
    qkv_s,
    qkv_r,
    cache_s,
    cache_r,
    o_s,
    o_r,
    z_s,
    z_r,
    y_s,
    y_r,
    x_s,
    x_r,
    f_s,
    f_r,
    m_s,
    m_r,
    out_s,
):
    s = lax.axis_index("seq")
    f = lax.axis_index("fsdp")
    z, y = s // 4, s % 4
    x, c = f // 2, f % 2
    even = (z + 1) % 2
    sigma = 1 - 2 * even
    base = (z // 2) * 2
    me = (z % 2) * 4 + y

    def at(dx=0, dy=0, dz=0):
        return (((z + dz) % 8) * 4 + (y + dy) % 4, ((x + dx) % 4) * 2 + c)

    partner = (s, x * 2 + (1 - c))

    def member(index):
        return ((base + index // 4) * 4 + index % 4, f)

    def remote(src, dst, ss, rs, device):
        return pltpu.make_async_remote_copy(
            src_ref=src, dst_ref=dst, send_sem=ss, recv_sem=rs, device_id=device, device_id_type=MESH
        )

    half = pl.ds(pl.multiple_of(c * 80, 16), 80)
    barrier = pltpu.get_barrier_semaphore()
    greeted = [partner, at(dx=1), at(dx=3)]
    greeted += [member((me + d) % 8) for d in range(1, 8)]
    greeted += [at(dz=sigma), at(dz=2 * sigma + 8), at(dz=3 * sigma + 8)]
    for device in greeted:
        pl.semaphore_signal(barrier, inc=1, device_id=device, device_id_type=MESH)
    staged = [
        pltpu.make_async_copy(src, dst, loc.at[1, n])
        for n, (src, dst) in enumerate(((q_hbm, q_ref), (k_hbm, k_ref), (v_hbm, v_ref)))
    ]
    for move in staged:
        move.start()
    raw_local = pltpu.make_async_copy(w_ref.at[half], pair.at[c], loc.at[0, 0])
    raw_local.start()
    pl.semaphore_wait(barrier, len(greeted))

    other = pl.ds(pl.multiple_of((1 - c) * 80, 16), 80)
    raw_remote = remote(w_ref.at[other], pair.at[c], one_s.at[0], one_r.at[0], partner)
    raw_remote.start()
    def pack(h):
        for index, ref in enumerate((q_ref, k_ref, v_ref)):

            for step in range(5):
                cols = pl.ds(step * 256, 256)
                from_cols = pl.ds(h * HALF + step * 256, 256)
                rows = jnp.dot(perm_ref[...], ref[:, from_cols], preferred_element_type=F32)
                send[h, :, index, :, cols] = rows.astype(BF16).reshape(8, 32, 256)

    raw_local.wait()
    raw_remote.wait()
    chunk = jnp.concatenate([pair[0].astype(F32), pair[1].astype(F32)], axis=1)

    def lanes(dx):
        return pl.ds(pl.multiple_of(((x + dx) % 4) * 640, 128), 640)

    wt[z, y, half, lanes(0)] = chunk.astype(BF16)

    def zof(i):
        rel = -((i + 1) // 2) if i % 2 else i // 2
        return (z + rel + 8) % 8

    def z_move(i, step):
        ref = wt.at[zof(i), y, half, lanes(0)]
        to_right = step[0] == "r"
        slot = step[1] + (0 if to_right else 4)
        return remote(ref, ref, z_s.at[slot], z_r.at[slot], at(dz=1 if to_right else 7))

    def y_move(i, kind):
        if kind == 0:
            ref, device = wt.at[zof(i), y, half, lanes(0)], at(dy=1)
        elif kind == 1:
            ref, device = wt.at[zof(i), y, half, lanes(0)], at(dy=3)
        else:
            ref, device = wt.at[zof(i), y, half, lanes(0)], at(dy=2)
        return remote(ref, ref, y_s.at[i, kind], y_r.at[i, kind], device)

    def x_move(i, kind):
        if kind == 0:
            ref, device = wt.at[zof(i), :, half, lanes(0)], at(dx=1)
        elif kind == 1:
            ref, device = wt.at[zof(i), :, half, lanes(0)], at(dx=3)
        elif kind == 2:
            ref, device = wt.at[zof(i), pl.ds(0, 2), half, lanes(3)], at(dx=1)
        else:
            ref, device = wt.at[zof(i), pl.ds(2, 2), half, lanes(1)], at(dx=3)
        return remote(ref, ref, x_s.at[i, kind], x_r.at[i, kind], device)

    def x_first(r, kind):
        row = (y + r) % 4
        if kind < 2:
            ref, device = wt.at[z, row, half, lanes(0)], at(dx=3 if kind else 1)
        elif r < 2:
            ref, device = wt.at[z, row, half, lanes(3)], at(dx=1)
        else:
            ref, device = wt.at[z, row, half, lanes(1)], at(dx=3)
        return remote(ref, ref, f_s.at[r, kind], f_r.at[r, kind], device)

    def last_mirror(n):
        rows = pl.ds(0, 2) if n == 3 else pl.ds(2, 2) if n == 4 else pl.ds(0, 4)
        ref = wt.at[zof(7), rows, half, lanes((0, 3, 1, 2, 2)[n])]
        return remote(ref, ref, m_s.at[7 + n], m_r.at[7 + n], partner)

    def mirror(i):
        ref = wt.at[zof(i), :, half]
        return remote(ref, ref, m_s.at[i], m_r.at[i], partner)

    x_first(0, 0).start()
    x_first(0, 1).start()
    z_move(0, ("r", 0)).start()
    z_move(0, ("l", 0)).start()
    for kind in range(3):
        y_move(0, kind).start()
    def exchange(h):
        moves = []
        lane_half = pl.ds(h * HALF, HALF)
        for j, off in ((1, sigma), (2, 8 - 2 * sigma), (3, 3 * sigma + 8)):
            to_z = (z + off + 8) % 8
            for n, ref in enumerate((ck_ref, cv_ref)):
                src = ref.at[to_z // 2, :, lane_half]
                sems = cache_s.at[h, j, n], cache_r.at[h, j, n]
                moves.append(remote(src, cache.at[h, j, n], *sems, (to_z * 4 + y, f)))
        for d in range(1, 8):
            to = (me + d) % 8
            sems = qkv_s.at[h, d], qkv_r.at[h, d]
            moves.append(remote(send.at[h, to], recv.at[h, me], *sems, member(to)))
        own = [pltpu.make_async_copy(send.at[h, me], recv.at[h, me], loc.at[h, 1])]
        for n, ref in enumerate((ck_ref, cv_ref)):
            src = ref.at[z // 2, :, lane_half]
            own.append(pltpu.make_async_copy(src, cache.at[h, 0, n], loc.at[h, 2 + n]))
        return moves, own

    exchanges = [exchange(0), exchange(1)]

    def start_exchange(h):
        if h:
            for move in exchanges[0][0]:
                move.wait_send()
        for move in exchanges[h][0] + exchanges[h][1]:
            move.start()

    def spatial(first, count):
        @pl.loop(first, first + count)
        def _(h):
            cols = pl.ds(pl.multiple_of(h * HD, HD), HD)
            scores = lax.dot_general(q_ref[:, cols], k_ref[:, cols], NT, preferred_element_type=F32)
            weights, inverse = softmax_parts(scores * SCALE2 + near_ref[...])
            values = jnp.dot(weights, v_ref[:, cols], preferred_element_type=F32)
            mixed[:, cols] = (values * inverse).astype(BF16)

    def z_steps(i):
        k = (i + 1) // 2
        if i % 2:
            z_move(i, ("r", k - 1)).wait_recv()
            if k < 4:
                z_move(i, ("r", k)).start()
        else:
            z_move(i, ("l", k - 1)).wait_recv()
            if k < 3:
                z_move(i, ("l", k)).start()
        y_move(i, 0).start()
        y_move(i, 1).start()
        y_move(i, 2).start()

    def y_steps(i):
        for kind, r in enumerate((3, 1, 2)):
            y_move(i, kind).wait_recv()
            if i == 0:
                x_first(r, 0).start()
                x_first(r, 1).start()
        if i:
            x_move(i, 0).start()
            x_move(i, 1).start()

    def x_steps(i):
        if i == 0:
            for r in (0, 3, 1, 2):
                x_first(r, 0).wait_recv()
                if r < 2:
                    x_first(r, 2).start()
                x_first(r, 1).wait_recv()
                if r >= 2:
                    x_first(r, 2).start()
            return
        x_move(i, 0).wait_recv()
        x_move(i, 2).start()
        if i == 7:
            last_mirror(1).start()
        x_move(i, 1).wait_recv()
        x_move(i, 3).start()
        if i == 7:
            last_mirror(2).start()

    def x_last(i):
        if i == 0:
            for r in range(4):
                x_first(r, 2).wait_recv()
        elif i == 7:
            last_mirror(0).start()
            x_move(i, 2).wait_recv()
            last_mirror(3).start()
            x_move(i, 3).wait_recv()
            last_mirror(4).start()
            return
        else:
            x_move(i, 2).wait_recv()
            x_move(i, 3).wait_recv()
        mirror(i).start()

    def o_exchange(h):
        moves = []
        for d in range(1, 8):
            to = (me + d) % 8
            sems = o_s.at[h, d], o_r.at[h, d]
            moves.append(remote(o_send.at[h, to], o_recv.at[h, me], *sems, member(to)))
        return moves, pltpu.make_async_copy(o_send.at[h, me], o_recv.at[h, me], loc.at[h, 4])

    o_exchanges = [o_exchange(0), o_exchange(1)]

    def temporal(h):
        moves, own = exchanges[h]
        for move in own:
            move.wait()
        for move in moves:
            move.wait_recv()

        for p in range(2):
            rows = pl.ds(p * 16, 16)
            slots = pl.ds(p * 2, 2)

            def head(cols):
                queries = recv[h, :, 0, rows, cols].reshape(128, HD)
                span_k = recv[h, :, 1, rows, cols].reshape(128, HD)
                span_v = recv[h, :, 2, rows, cols].reshape(128, HD)
                old_k = cache[h, slots, 0, :, cols].reshape(128, HD)
                old_v = cache[h, slots, 1, :, cols].reshape(128, HD)
                keys = jnp.concatenate([span_k, old_k], axis=0)
                values = jnp.concatenate([span_v, old_v], axis=0)
                scores = lax.dot_general(queries, keys, NT, preferred_element_type=F32)
                weights, inverse = softmax_parts(scores * SCALE2 + live_ref[...])
                result = jnp.dot(weights, values, preferred_element_type=F32) * inverse
                o_send[h, :, rows, cols] = result.astype(BF16).reshape(8, 16, HD)

            @pl.loop(0, 10 // TEMPORAL_UNROLL)
            def _(step, head=head):
                for n in range(TEMPORAL_UNROLL):
                    head(pl.ds(pl.multiple_of((step * TEMPORAL_UNROLL + n) * HD, HD), HD))

        moves, own = o_exchanges[h]
        for move in moves:
            move.start()
        own.start()

    def combine(h):
        moves, own = o_exchanges[h]
        own.wait()
        for move in moves:
            move.wait_recv()

        for step in range(5):
            cols = pl.ds(step * 256, 256)
            to_cols = pl.ds(h * HALF + step * 256, 256)
            rows = jnp.dot(
                back_ref[...], o_recv[h, :, :, cols].reshape(256, 256), preferred_element_type=F32
            )
            mixed[:, to_cols] = (mixed[:, to_cols].astype(F32) + rows).astype(BF16)

    def out_move(i):
        cols = pl.ds(pl.multiple_of(zof(i) * 640, 128), 640)
        return pltpu.make_async_copy(out_buf.at[i % 2], out_ref.at[:, cols], out_s.at[i % 2])

    def project(i, h):
        lane_half = pl.ds(h * HALF, HALF)
        if h == 0 and i < 7:
            mirror(i).wait_recv()
        elif h == 0:
            for n in range(5):
                last_mirror(n).wait_recv()
        block = wt[zof(i), :, :, lane_half].reshape(640, HALF)
        result = lax.dot_general(mixed[:, lane_half], block, NT, preferred_element_type=F32)
        if h == 0:
            total[i] = result
        else:
            if i > 1:
                out_move(i - 2).wait()
            out_buf[i % 2] = (result + total[i]).astype(BF16)
            out_move(i).start()

    def run(step):
        kind, index = step[0], int(step[1:])
        if kind == "b":
            for move in staged:
                move.wait()
            tables(
                z, order_ref, near_tiles_ref, frames_ref, perm_ref, back_ref, near_ref, live_ref
            )
        elif kind == "z":
            z_steps(index)
        elif kind == "y":
            y_steps(index)
        elif kind == "x":
            x_steps(index)
        elif kind == "l":
            x_last(index)
        elif kind == "s":
            spatial(index * 4, 4)
        elif kind == "k":
            pack(index)
        elif kind == "a":
            start_exchange(index)
        elif kind == "t":
            temporal(index)
        elif kind == "c":
            combine(index)
        elif kind == "p":
            project(index % 10, index // 10)

    for step in SCHEDULE:
        run(step)
    out_move(6).wait()
    out_move(7).wait()

    for h in range(2):
        for move in (exchanges[h][0] if h else []) + o_exchanges[h][0]:
            move.wait_send()
    for k in range(4):
        z_move(0, ("r", k)).wait_send()
    for k in range(3):
        z_move(0, ("l", k)).wait_send()
    for i in range(8):
        for kind in range(3):
            y_move(i, kind).wait_send()
        for kind in range(4 if i else 0):
            x_move(i, kind).wait_send()
        if i < 7:
            mirror(i).wait_send()
    for r in range(4):
        for kind in range(3):
            x_first(r, kind).wait_send()
    for n in range(5):
        last_mirror(n).wait_send()


def shards(queries, key_rows, value_rows, cache_keys, cache_values, cache_frames, neighbors, tile_order, out_weight):
    vmem = pl.BlockSpec(memory_space=pltpu.VMEM)
    hbm = pl.BlockSpec(memory_space=pl.ANY)
    dma = pltpu.SemaphoreType.DMA
    out = pl.pallas_call(
        kernel,
        out_shape=jax.ShapeDtypeStruct((256, D), BF16),
        in_specs=[hbm] * 3 + [vmem] * 2 + [pl.BlockSpec(memory_space=pltpu.SMEM)] + [hbm] * 3,
        out_specs=hbm,
        scratch_shapes=[
            pltpu.VMEM((2, 8, 3, 32, HALF), BF16),
            pltpu.VMEM((2, 8, 3, 32, HALF), BF16),
            pltpu.VMEM((2, 4, 2, 64, HALF), BF16),
            pltpu.VMEM((2, 8, 32, HALF), BF16),
            pltpu.VMEM((2, 8, 32, HALF), BF16),
            pltpu.VMEM((256, HH), BF16),
            pltpu.VMEM((256, HH), BF16),
            pltpu.VMEM((256, HH), BF16),
            pltpu.VMEM((256, HH), BF16),
            pltpu.VMEM((256, 256), BF16),
            pltpu.VMEM((256, 256), BF16),
            pltpu.VMEM((256, 256), F32),
            pltpu.VMEM((128, 256), F32),
            pltpu.VMEM((2, 80, 320), BF16),
            pltpu.VMEM((8, 4, 160, HH), BF16),
            pltpu.VMEM((2, 256, 640), BF16),
            pltpu.VMEM((8, 256, 640), F32),
            dma((1,)),
            dma((1,)),
            dma((2, 5)),
            dma((2, 8)),
            dma((2, 8)),
            dma((2, 4, 2)),
            dma((2, 4, 2)),
            dma((2, 8)),
            dma((2, 8)),
            dma((8,)),
            dma((8,)),
            dma((8, 3)),
            dma((8, 3)),
            dma((8, 4)),
            dma((8, 4)),
            dma((4, 3)),
            dma((4, 3)),
            dma((12,)),
            dma((12,)),
            dma((2,)),
        ],
        compiler_params=pltpu.CompilerParams(
            collective_id=0, has_side_effects=True, vmem_limit_bytes=60 * 2**20
        ),
        cost_estimate=pl.CostEstimate(flops=9 * 10**9, bytes_accessed=2 * 10**7, transcendentals=3 * 10**6),
    )(
        queries.reshape(256, HH),
        key_rows.reshape(256, HH),
        value_rows.reshape(256, HH),
        tile_order.reshape(1, 32),
        neighbors.T,
        cache_frames.T,
        cache_keys.reshape(4, 64, HH),
        cache_values.reshape(4, 64, HH),
        out_weight.T,
    )
    return out.reshape(1, 1, 256, D)


def solution(mesh):
    placed = (
        P("seq", "fsdp", None, None),
        P("seq", "fsdp", None, None),
        P("seq", "fsdp", None, None),
        P("seq", None, "fsdp", None, None),
        P("seq", None, "fsdp", None, None),
        P(None, "fsdp"),
        P(),
        P(),
        P("fsdp", "seq"),
    )
    return jax.shard_map(
        shards, mesh=mesh, in_specs=placed, out_specs=P("seq", "fsdp", None, None), check_vma=False
    )
```

```python
import functools

import jax
import jax.numpy as jnp
from jax import lax
from jax.experimental import pallas as pl
from jax.experimental.pallas import tpu as pltpu
from jax.sharding import PartitionSpec as P

MESH = pl.DeviceIdType.MESH
HEADS = 20
HD = 128
TILE = 8
CACHE = 8
HH = 2560
HALF = 1280
TEMPORAL_UNROLL = 5
SCHEDULE = ('z1', 'z2', 'y0', 'b0', 'z3', 'z4', 'y1', 'k0', 'z5', 'z6', 'y2', 'z7', 'a0', 'x0', 'k1', 's0', 'y3', 's1', 'y7', 'y4', 's2', 'x1', 'y5', 's3', 'y6', 's4', 'x2', 'a1', 't0', 'x3', 'x4', 'x5', 'x7', 'x6', 'l0', 'l1', 'l2', 'l3', 'l7', 'l4', 'l5', 't1', 'l6', 'c0', 'p0', 'p1', 'p2', 'p3', 'p4', 'p5', 'p7', 'p6', 'c1', 'p10', 'p11', 'p12', 'p13', 'p14', 'p15', 'p17', 'p16')
D = 5120
BF16 = jnp.bfloat16
F32 = jnp.float32
NEG = -1e30
LOG2E = 1.4426950408889634
SCALE2 = HD ** (-0.5) * LOG2E
NT = (((1,), (1,)), ((), ()))


def softmax_parts(scores):
    top = jnp.max(scores, axis=-1, keepdims=True)
    weights = jnp.exp2(scores - top)
    total = jnp.sum(weights, axis=-1, keepdims=True)
    return weights.astype(BF16), 1.0 / total


def tables(z, order_ref, near_tiles_ref, frames_ref, perm_ref, back_ref, near_ref, live_ref):
    def iota(shape, dim):
        return lax.broadcasted_iota(jnp.int32, shape, dim)

    def slot_of(token):
        index, j = token >> 5, (token >> 3) & 3
        side = index >> 2
        return ((((z // 2) * 2 + side + j * (2 * side - 1) + 8) & 7) << 2) + (index & 3)

    order = order_ref[...]
    held = iota((256, 32), 1) == slot_of(iota((256, 32), 0))
    tile = jnp.sum(jnp.where(held, jnp.broadcast_to(order, (256, 32)), 0), axis=1, keepdims=True)
    source = tile * 8 + (iota((256, 1), 0) & 7)
    perm_ref[...] = jnp.where(source == iota((256, 256), 1), 1.0, 0.0).astype(BF16)
    held = iota((32, 256), 0) == slot_of(iota((32, 256), 1))
    tile = jnp.dot(
        jnp.broadcast_to(order, (8, 32)).astype(F32).astype(BF16),
        jnp.where(held, 1.0, 0.0).astype(BF16),
        preferred_element_type=F32,
    )[:1].astype(jnp.int32)
    source = tile * 8 + (iota((1, 256), 1) & 7)
    back_ref[...] = jnp.where(source == iota((256, 256), 0), 1.0, 0.0).astype(BF16)

    mine = iota((256, 32), 1) == iota((256, 32), 0) >> 3
    tiles = lax.dot_general(
        jnp.where(mine, 1.0, 0.0).astype(BF16),
        near_tiles_ref[...].astype(F32).astype(BF16),
        NT,
        preferred_element_type=F32,
    ).astype(jnp.int32)
    column = iota((256, 256), 1) >> 3
    near = tiles[:, 0:1] == column
    for n in range(1, 9):
        near = near | (tiles[:, n : n + 1] == column)
    near_ref[...] = jnp.where(near, 0.0, NEG)

    row, col = iota((128, 256), 0), iota((128, 256), 1)
    side = (row >> 3) & 1
    span = (col < 128) & (side == (col >> 3) & 1) & (col >> 4 <= row >> 4)
    old = (col >= 128) & (side == (col >> 6) & 1)
    old = old & ((col >> 3) & 7 >= CACHE - frames_ref[0, z // 2])
    live_ref[...] = jnp.where(span | old, 0.0, NEG)


def kernel(
    q_hbm,
    k_hbm,
    v_hbm,
    order_ref,
    near_tiles_ref,
    frames_ref,
    ck_ref,
    cv_ref,
    w_ref,
    out_ref,
    send,
    recv,
    cache,
    o_send,
    o_recv,
    mixed,
    q_ref,
    k_ref,
    v_ref,
    perm_ref,
    back_ref,
    near_ref,
    live_ref,
    pair,
    wt,
    out_buf,
    total,
    one_s,
    one_r,
    loc,
    qkv_s,
    qkv_r,
    cache_s,
    cache_r,
    o_s,
    o_r,
    z_s,
    z_r,
    y_s,
    y_r,
    x_s,
    x_r,
    f_s,
    f_r,
    m_s,
    m_r,
    out_s,
):
    s = lax.axis_index("seq")
    f = lax.axis_index("fsdp")
    z, y = s // 4, s % 4
    x, c = f // 2, f % 2
    even = (z + 1) % 2
    sigma = 1 - 2 * even
    base = (z // 2) * 2
    me = (z % 2) * 4 + y

    def at(dx=0, dy=0, dz=0):
        return (((z + dz) % 8) * 4 + (y + dy) % 4, ((x + dx) % 4) * 2 + c)

    partner = (s, x * 2 + (1 - c))

    def member(index):
        return ((base + index // 4) * 4 + index % 4, f)

    def remote(src, dst, ss, rs, device):
        return pltpu.make_async_remote_copy(
            src_ref=src, dst_ref=dst, send_sem=ss, recv_sem=rs, device_id=device, device_id_type=MESH
        )

    half = pl.ds(pl.multiple_of(c * 80, 16), 80)
    barrier = pltpu.get_barrier_semaphore()
    greeted = [partner, at(dx=1), at(dx=2), at(dx=3)]
    greeted += [member((me + d) % 8) for d in range(1, 8)]
    greeted += [at(dz=sigma), at(dz=2 * sigma + 8), at(dz=3 * sigma + 8)]
    for device in greeted:
        pl.semaphore_signal(barrier, inc=1, device_id=device, device_id_type=MESH)
    staged = [
        pltpu.make_async_copy(src, dst, loc.at[1, n])
        for n, (src, dst) in enumerate(((q_hbm, q_ref), (k_hbm, k_ref), (v_hbm, v_ref)))
    ]
    for move in staged:
        move.start()
    raw_local = pltpu.make_async_copy(w_ref.at[half], pair.at[c], loc.at[0, 0])
    raw_local.start()
    pl.semaphore_wait(barrier, len(greeted))

    other = pl.ds(pl.multiple_of((1 - c) * 80, 16), 80)
    raw_remote = remote(w_ref.at[other], pair.at[c], one_s.at[0], one_r.at[0], partner)
    raw_remote.start()
    def pack(h):
        for index, ref in enumerate((q_ref, k_ref, v_ref)):

            for step in range(5):
                cols = pl.ds(step * 256, 256)
                from_cols = pl.ds(h * HALF + step * 256, 256)
                rows = jnp.dot(perm_ref[...], ref[:, from_cols], preferred_element_type=F32)
                send[h, :, index, :, cols] = rows.astype(BF16).reshape(8, 32, 256)

    raw_local.wait()
    raw_remote.wait()
    chunk = jnp.concatenate([pair[0].astype(F32), pair[1].astype(F32)], axis=1)

    def lanes(dx):
        return pl.ds(pl.multiple_of(((x + dx) % 4) * 640, 128), 640)

    wt[z, y, half, lanes(0)] = chunk.astype(BF16)

    def zof(i):
        rel = -((i + 1) // 2) if i % 2 else i // 2
        return (z + rel + 8) % 8

    def z_move(i, step):
        ref = wt.at[zof(i), y, half, lanes(0)]
        to_right = step[0] == "r"
        slot = step[1] + (0 if to_right else 4)
        return remote(ref, ref, z_s.at[slot], z_r.at[slot], at(dz=1 if to_right else 7))

    def y_move(i, kind):
        if i == 7:
            ref, device = wt.at[zof(i), y, half, lanes(0)], at(dx=(1, 3, 2)[kind])
        elif kind == 0:
            ref, device = wt.at[zof(i), y, half, lanes(0)], at(dy=1)
        elif kind == 1:
            ref, device = wt.at[zof(i), y, half, lanes(0)], at(dy=3)
        else:
            ref, device = wt.at[zof(i), y, half, lanes(0)], at(dy=2)
        return remote(ref, ref, y_s.at[i, kind], y_r.at[i, kind], device)

    def x_move(i, kind):
        if i == 7:
            row = (y + (0, 0, 3, 1)[kind]) % 4
            part = (pl.ds(0, HH), pl.ds(0, HH), pl.ds(0, HALF), pl.ds(HALF, HALF))[kind]
            ref, device = wt.at[zof(i), row, half, part], at(dy=(1, 3, 1, 3)[kind])
        elif kind == 0:
            ref, device = wt.at[zof(i), :, half, lanes(0)], at(dx=1)
        elif kind == 1:
            ref, device = wt.at[zof(i), :, half, lanes(0)], at(dx=3)
        elif kind == 2:
            ref, device = wt.at[zof(i), pl.ds(0, 2), half, lanes(3)], at(dx=1)
        else:
            ref, device = wt.at[zof(i), pl.ds(2, 2), half, lanes(1)], at(dx=3)
        return remote(ref, ref, x_s.at[i, kind], x_r.at[i, kind], device)

    def x_first(r, kind):
        row = (y + r) % 4
        if kind < 2:
            ref, device = wt.at[z, row, half, lanes(0)], at(dx=3 if kind else 1)
        elif r < 2:
            ref, device = wt.at[z, row, half, lanes(3)], at(dx=1)
        else:
            ref, device = wt.at[z, row, half, lanes(1)], at(dx=3)
        return remote(ref, ref, f_s.at[r, kind], f_r.at[r, kind], device)

    def last_mirror(n):
        if n < 5:
            rows = pl.ds(0, 2) if n == 3 else pl.ds(2, 2) if n == 4 else pl.ds(0, 4)
            ref = wt.at[zof(6), rows, half, lanes((0, 3, 1, 2, 2)[n])]
        else:
            ref = wt.at[zof(7), (y + (0, 3, 1, 2)[n - 5]) % 4, half]
        return remote(ref, ref, m_s.at[6 + n], m_r.at[6 + n], partner)

    def mirror(i):
        ref = wt.at[zof(i), :, half]
        return remote(ref, ref, m_s.at[i], m_r.at[i], partner)

    x_first(0, 0).start()
    x_first(0, 1).start()
    z_move(0, ("r", 0)).start()
    z_move(0, ("l", 0)).start()
    for kind in range(3):
        y_move(0, kind).start()
    def exchange(h):
        moves = []
        lane_half = pl.ds(h * HALF, HALF)
        for j, off in ((1, sigma), (2, 8 - 2 * sigma), (3, 3 * sigma + 8)):
            to_z = (z + off + 8) % 8
            for n, ref in enumerate((ck_ref, cv_ref)):
                src = ref.at[to_z // 2, :, lane_half]
                sems = cache_s.at[h, j, n], cache_r.at[h, j, n]
                moves.append(remote(src, cache.at[h, j, n], *sems, (to_z * 4 + y, f)))
        for d in range(1, 8):
            to = (me + d) % 8
            sems = qkv_s.at[h, d], qkv_r.at[h, d]
            moves.append(remote(send.at[h, to], recv.at[h, me], *sems, member(to)))
        own = [pltpu.make_async_copy(send.at[h, me], recv.at[h, me], loc.at[h, 1])]
        for n, ref in enumerate((ck_ref, cv_ref)):
            src = ref.at[z // 2, :, lane_half]
            own.append(pltpu.make_async_copy(src, cache.at[h, 0, n], loc.at[h, 2 + n]))
        return moves, own

    exchanges = [exchange(0), exchange(1)]

    def start_exchange(h):
        if h:
            for move in exchanges[0][0]:
                move.wait_send()
        for move in exchanges[h][0] + exchanges[h][1]:
            move.start()

    def spatial(first, count):
        @pl.loop(first, first + count)
        def _(h):
            cols = pl.ds(pl.multiple_of(h * HD, HD), HD)
            scores = lax.dot_general(q_ref[:, cols], k_ref[:, cols], NT, preferred_element_type=F32)
            weights, inverse = softmax_parts(scores * SCALE2 + near_ref[...])
            values = jnp.dot(weights, v_ref[:, cols], preferred_element_type=F32)
            mixed[:, cols] = (values * inverse).astype(BF16)

    def z_steps(i):
        k = (i + 1) // 2
        if i % 2:
            z_move(i, ("r", k - 1)).wait_recv()
            if k < 4:
                z_move(i, ("r", k)).start()
        else:
            z_move(i, ("l", k - 1)).wait_recv()
            if k < 3:
                z_move(i, ("l", k)).start()
        y_move(i, 0).start()
        y_move(i, 1).start()
        y_move(i, 2).start()

    def y_steps(i):
        for kind, r in enumerate((3, 1, 2)):
            y_move(i, kind).wait_recv()
            if i == 0:
                x_first(r, 0).start()
                x_first(r, 1).start()
        if i:
            x_move(i, 0).start()
            x_move(i, 1).start()

    def x_steps(i):
        if i == 0:
            for r in (0, 3, 1, 2):
                x_first(r, 0).wait_recv()
                if r < 2:
                    x_first(r, 2).start()
                x_first(r, 1).wait_recv()
                if r >= 2:
                    x_first(r, 2).start()
            return
        x_move(i, 0).wait_recv()
        x_move(i, 2).start()
        if i >= 6:
            last_mirror(1 if i == 6 else 6).start()
        x_move(i, 1).wait_recv()
        x_move(i, 3).start()
        if i >= 6:
            last_mirror(2 if i == 6 else 7).start()

    def x_last(i):
        if i == 0:
            for r in range(4):
                x_first(r, 2).wait_recv()
        elif i == 7:
            last_mirror(5).start()
            x_move(i, 2).wait_recv()
            x_move(i, 3).wait_recv()
            last_mirror(8).start()
            return
        elif i == 6:
            last_mirror(0).start()
            x_move(i, 2).wait_recv()
            last_mirror(3).start()
            x_move(i, 3).wait_recv()
            last_mirror(4).start()
            return
        else:
            x_move(i, 2).wait_recv()
            x_move(i, 3).wait_recv()
        mirror(i).start()

    def o_exchange(h):
        moves = []
        for d in range(1, 8):
            to = (me + d) % 8
            sems = o_s.at[h, d], o_r.at[h, d]
            moves.append(remote(o_send.at[h, to], o_recv.at[h, me], *sems, member(to)))
        return moves, pltpu.make_async_copy(o_send.at[h, me], o_recv.at[h, me], loc.at[h, 4])

    o_exchanges = [o_exchange(0), o_exchange(1)]

    def temporal(h):
        moves, own = exchanges[h]
        for move in own:
            move.wait()
        for move in moves:
            move.wait_recv()

        for p in range(2):
            rows = pl.ds(p * 16, 16)
            slots = pl.ds(p * 2, 2)

            def head(cols):
                queries = recv[h, :, 0, rows, cols].reshape(128, HD)
                span_k = recv[h, :, 1, rows, cols].reshape(128, HD)
                span_v = recv[h, :, 2, rows, cols].reshape(128, HD)
                old_k = cache[h, slots, 0, :, cols].reshape(128, HD)
                old_v = cache[h, slots, 1, :, cols].reshape(128, HD)
                keys = jnp.concatenate([span_k, old_k], axis=0)
                values = jnp.concatenate([span_v, old_v], axis=0)
                scores = lax.dot_general(queries, keys, NT, preferred_element_type=F32)
                weights, inverse = softmax_parts(scores * SCALE2 + live_ref[...])
                result = jnp.dot(weights, values, preferred_element_type=F32) * inverse
                o_send[h, :, rows, cols] = result.astype(BF16).reshape(8, 16, HD)

            @pl.loop(0, 10 // TEMPORAL_UNROLL)
            def _(step, head=head):
                for n in range(TEMPORAL_UNROLL):
                    head(pl.ds(pl.multiple_of((step * TEMPORAL_UNROLL + n) * HD, HD), HD))

        moves, own = o_exchanges[h]
        for move in moves:
            move.start()
        own.start()

    def combine(h):
        moves, own = o_exchanges[h]
        own.wait()
        for move in moves:
            move.wait_recv()

        for step in range(5):
            cols = pl.ds(step * 256, 256)
            to_cols = pl.ds(h * HALF + step * 256, 256)
            rows = jnp.dot(
                back_ref[...], o_recv[h, :, :, cols].reshape(256, 256), preferred_element_type=F32
            )
            mixed[:, to_cols] = (mixed[:, to_cols].astype(F32) + rows).astype(BF16)

    def out_move(i):
        cols = pl.ds(pl.multiple_of(zof(i) * 640, 128), 640)
        return pltpu.make_async_copy(out_buf.at[i % 2], out_ref.at[:, cols], out_s.at[i % 2])

    def project(i, h):
        lane_half = pl.ds(h * HALF, HALF)
        if h == 0 and i < 6:
            mirror(i).wait_recv()
        elif h == 0:
            for n in range(5) if i == 6 else range(5, 9):
                last_mirror(n).wait_recv()
        block = wt[zof(i), :, :, lane_half].reshape(640, HALF)
        result = lax.dot_general(mixed[:, lane_half], block, NT, preferred_element_type=F32)
        if h == 0:
            total[i] = result
        else:
            if i > 1:
                out_move(i - 2).wait()
            out_buf[i % 2] = (result + total[i]).astype(BF16)
            out_move(i).start()

    def run(step):
        kind, index = step[0], int(step[1:])
        if kind == "b":
            for move in staged:
                move.wait()
            tables(
                z, order_ref, near_tiles_ref, frames_ref, perm_ref, back_ref, near_ref, live_ref
            )
        elif kind == "z":
            z_steps(index)
        elif kind == "y":
            y_steps(index)
        elif kind == "x":
            x_steps(index)
        elif kind == "l":
            x_last(index)
        elif kind == "s":
            spatial(index * 4, 4)
        elif kind == "k":
            pack(index)
        elif kind == "a":
            start_exchange(index)
        elif kind == "t":
            temporal(index)
        elif kind == "c":
            combine(index)
        elif kind == "p":
            project(index % 10, index // 10)

    for step in SCHEDULE:
        run(step)
    out_move(6).wait()
    out_move(7).wait()

    for h in range(2):
        for move in (exchanges[h][0] if h else []) + o_exchanges[h][0]:
            move.wait_send()
    for k in range(4):
        z_move(0, ("r", k)).wait_send()
    for k in range(3):
        z_move(0, ("l", k)).wait_send()
    for i in range(8):
        for kind in range(3):
            y_move(i, kind).wait_send()
        for kind in range(4 if i else 0):
            x_move(i, kind).wait_send()
        if i < 6:
            mirror(i).wait_send()
    for r in range(4):
        for kind in range(3):
            x_first(r, kind).wait_send()
    for n in range(9):
        last_mirror(n).wait_send()


def shards(queries, key_rows, value_rows, cache_keys, cache_values, cache_frames, neighbors, tile_order, out_weight):
    vmem = pl.BlockSpec(memory_space=pltpu.VMEM)
    hbm = pl.BlockSpec(memory_space=pl.ANY)
    dma = pltpu.SemaphoreType.DMA
    out = pl.pallas_call(
        kernel,
        out_shape=jax.ShapeDtypeStruct((256, D), BF16),
        in_specs=[hbm] * 3 + [vmem] * 2 + [pl.BlockSpec(memory_space=pltpu.SMEM)] + [hbm] * 3,
        out_specs=hbm,
        scratch_shapes=[
            pltpu.VMEM((2, 8, 3, 32, HALF), BF16),
            pltpu.VMEM((2, 8, 3, 32, HALF), BF16),
            pltpu.VMEM((2, 4, 2, 64, HALF), BF16),
            pltpu.VMEM((2, 8, 32, HALF), BF16),
            pltpu.VMEM((2, 8, 32, HALF), BF16),
            pltpu.VMEM((256, HH), BF16),
            pltpu.VMEM((256, HH), BF16),
            pltpu.VMEM((256, HH), BF16),
            pltpu.VMEM((256, HH), BF16),
            pltpu.VMEM((256, 256), BF16),
            pltpu.VMEM((256, 256), BF16),
            pltpu.VMEM((256, 256), F32),
            pltpu.VMEM((128, 256), F32),
            pltpu.VMEM((2, 80, 320), BF16),
            pltpu.VMEM((8, 4, 160, HH), BF16),
            pltpu.VMEM((2, 256, 640), BF16),
            pltpu.VMEM((8, 256, 640), F32),
            dma((1,)),
            dma((1,)),
            dma((2, 5)),
            dma((2, 8)),
            dma((2, 8)),
            dma((2, 4, 2)),
            dma((2, 4, 2)),
            dma((2, 8)),
            dma((2, 8)),
            dma((8,)),
            dma((8,)),
            dma((8, 3)),
            dma((8, 3)),
            dma((8, 4)),
            dma((8, 4)),
            dma((4, 3)),
            dma((4, 3)),
            dma((15,)),
            dma((15,)),
            dma((2,)),
        ],
        compiler_params=pltpu.CompilerParams(
            collective_id=0, has_side_effects=True, vmem_limit_bytes=60 * 2**20
        ),
        cost_estimate=pl.CostEstimate(flops=9 * 10**9, bytes_accessed=2 * 10**7, transcendentals=3 * 10**6),
    )(
        queries.reshape(256, HH),
        key_rows.reshape(256, HH),
        value_rows.reshape(256, HH),
        tile_order.reshape(1, 32),
        neighbors.T,
        cache_frames.T,
        cache_keys.reshape(4, 64, HH),
        cache_values.reshape(4, 64, HH),
        out_weight.T,
    )
    return out.reshape(1, 1, 256, D)


def solution(mesh):
    placed = (
        P("seq", "fsdp", None, None),
        P("seq", "fsdp", None, None),
        P("seq", "fsdp", None, None),
        P("seq", None, "fsdp", None, None),
        P("seq", None, "fsdp", None, None),
        P(None, "fsdp"),
        P(),
        P(),
        P("fsdp", "seq"),
    )
    return jax.shard_map(
        shards, mesh=mesh, in_specs=placed, out_specs=P("seq", "fsdp", None, None), check_vma=False
    )
```

```python
import functools

import jax
import jax.numpy as jnp
from jax import lax
from jax.experimental import pallas as pl
from jax.experimental.pallas import tpu as pltpu
from jax.sharding import PartitionSpec as P

MESH = pl.DeviceIdType.MESH
HEADS = 20
HD = 128
TILE = 8
CACHE = 8
HH = 2560
HALF = 1280
TEMPORAL_UNROLL = 10
SCHEDULE = ('z1', 'z2', 'y0', 'z3', 'z4', 'b0', 'y1', 'z5', 'z6', 'k0', 'y2', 'z7', 'a0', 'x0', 'k1', 's0', 'y3', 's1', 'y7', 'y4', 's2', 'x1', 'y5', 's3', 'y6', 's4', 'x2', 'a1', 't0', 'x3', 'x4', 'x5', 'x7', 'x6', 'l0', 'l1', 'l2', 'l3', 'l7', 'l4', 'l5', 't1', 'l6', 'c0', 'p0', 'p1', 'p2', 'p3', 'p4', 'p5', 'p7', 'p6', 'c1', 'p10', 'p11', 'p12', 'p13', 'p14', 'p15', 'p17', 'p16')
D = 5120
BF16 = jnp.bfloat16
F32 = jnp.float32
NEG = -1e30
LOG2E = 1.4426950408889634
SCALE2 = HD ** (-0.5) * LOG2E
NT = (((1,), (1,)), ((), ()))


def softmax_parts(scores):
    top = jnp.max(scores, axis=-1, keepdims=True)
    weights = jnp.exp2(scores - top)
    total = jnp.sum(weights, axis=-1, keepdims=True)
    return weights.astype(BF16), 1.0 / total


def tables(z, order_ref, near_tiles_ref, frames_ref, perm_ref, back_ref, near_ref, live_ref):
    def iota(shape, dim):
        return lax.broadcasted_iota(jnp.int32, shape, dim)

    def slot_of(token):
        index, j = token >> 5, (token >> 3) & 3
        side = index >> 2
        return ((((z // 2) * 2 + side + j * (2 * side - 1) + 8) & 7) << 2) + (index & 3)

    order = order_ref[...]
    held = iota((256, 32), 1) == slot_of(iota((256, 32), 0))
    tile = jnp.sum(jnp.where(held, jnp.broadcast_to(order, (256, 32)), 0), axis=1, keepdims=True)
    source = tile * 8 + (iota((256, 1), 0) & 7)
    perm_ref[...] = jnp.where(source == iota((256, 256), 1), 1.0, 0.0).astype(BF16)
    held = iota((32, 256), 0) == slot_of(iota((32, 256), 1))
    tile = jnp.dot(
        jnp.broadcast_to(order, (8, 32)).astype(F32).astype(BF16),
        jnp.where(held, 1.0, 0.0).astype(BF16),
        preferred_element_type=F32,
    )[:1].astype(jnp.int32)
    source = tile * 8 + (iota((1, 256), 1) & 7)
    back_ref[...] = jnp.where(source == iota((256, 256), 0), 1.0, 0.0).astype(BF16)

    mine = iota((256, 32), 1) == iota((256, 32), 0) >> 3
    tiles = lax.dot_general(
        jnp.where(mine, 1.0, 0.0).astype(BF16),
        near_tiles_ref[...].astype(F32).astype(BF16),
        NT,
        preferred_element_type=F32,
    ).astype(jnp.int32)
    column = iota((256, 256), 1) >> 3
    near = tiles[:, 0:1] == column
    for n in range(1, 9):
        near = near | (tiles[:, n : n + 1] == column)
    near_ref[...] = jnp.where(near, 0.0, NEG)

    row, col = iota((128, 256), 0), iota((128, 256), 1)
    side = (row >> 3) & 1
    span = (col < 128) & (side == (col >> 3) & 1) & (col >> 4 <= row >> 4)
    old = (col >= 128) & (side == (col >> 6) & 1)
    old = old & ((col >> 3) & 7 >= CACHE - frames_ref[0, z // 2])
    live_ref[...] = jnp.where(span | old, 0.0, NEG)


def kernel(
    q_hbm,
    k_hbm,
    v_hbm,
    order_ref,
    near_tiles_ref,
    frames_ref,
    ck_ref,
    cv_ref,
    w_ref,
    out_ref,
    send,
    recv,
    cache,
    o_send,
    o_recv,
    mixed,
    q_ref,
    k_ref,
    v_ref,
    perm_ref,
    back_ref,
    near_ref,
    live_ref,
    pair,
    wt,
    out_buf,
    total,
    one_s,
    one_r,
    loc,
    qkv_s,
    qkv_r,
    cache_s,
    cache_r,
    o_s,
    o_r,
    z_s,
    z_r,
    y_s,
    y_r,
    x_s,
    x_r,
    f_s,
    f_r,
    m_s,
    m_r,
    out_s,
):
    s = lax.axis_index("seq")
    f = lax.axis_index("fsdp")
    z, y = s // 4, s % 4
    x, c = f // 2, f % 2
    even = (z + 1) % 2
    sigma = 1 - 2 * even
    base = (z // 2) * 2
    me = (z % 2) * 4 + y

    def at(dx=0, dy=0, dz=0):
        return (((z + dz) % 8) * 4 + (y + dy) % 4, ((x + dx) % 4) * 2 + c)

    partner = (s, x * 2 + (1 - c))

    def member(index):
        return ((base + index // 4) * 4 + index % 4, f)

    def remote(src, dst, ss, rs, device):
        return pltpu.make_async_remote_copy(
            src_ref=src, dst_ref=dst, send_sem=ss, recv_sem=rs, device_id=device, device_id_type=MESH
        )

    half = pl.ds(pl.multiple_of(c * 80, 16), 80)
    barrier = pltpu.get_barrier_semaphore()
    greeted = [partner, at(dx=1), at(dx=2), at(dx=3)]
    greeted += [member((me + d) % 8) for d in range(1, 8)]
    greeted += [at(dz=sigma), at(dz=2 * sigma + 8), at(dz=3 * sigma + 8)]
    for device in greeted:
        pl.semaphore_signal(barrier, inc=1, device_id=device, device_id_type=MESH)
    staged = [
        pltpu.make_async_copy(src, dst, loc.at[1, n])
        for n, (src, dst) in enumerate(((q_hbm, q_ref), (k_hbm, k_ref), (v_hbm, v_ref)))
    ]
    for move in staged:
        move.start()
    raw_local = pltpu.make_async_copy(w_ref.at[half], pair.at[c], loc.at[0, 0])
    raw_local.start()
    pl.semaphore_wait(barrier, len(greeted))

    other = pl.ds(pl.multiple_of((1 - c) * 80, 16), 80)
    raw_remote = remote(w_ref.at[other], pair.at[c], one_s.at[0], one_r.at[0], partner)
    raw_remote.start()
    def pack(h):
        for index, ref in enumerate((q_ref, k_ref, v_ref)):

            for step in range(5):
                cols = pl.ds(step * 256, 256)
                from_cols = pl.ds(h * HALF + step * 256, 256)
                rows = jnp.dot(perm_ref[...], ref[:, from_cols], preferred_element_type=F32)
                send[h, :, index, :, cols] = rows.astype(BF16).reshape(8, 32, 256)

    raw_local.wait()
    raw_remote.wait()
    chunk = jnp.concatenate([pair[0].astype(F32), pair[1].astype(F32)], axis=1)

    def lanes(dx):
        return pl.ds(pl.multiple_of(((x + dx) % 4) * 640, 128), 640)

    wt[z, y, half, lanes(0)] = chunk.astype(BF16)

    def zof(i):
        rel = -((i + 1) // 2) if i % 2 else i // 2
        return (z + rel + 8) % 8

    def z_move(i, step):
        ref = wt.at[zof(i), y, half, lanes(0)]
        to_right = step[0] == "r"
        slot = step[1] + (0 if to_right else 4)
        return remote(ref, ref, z_s.at[slot], z_r.at[slot], at(dz=1 if to_right else 7))

    def y_move(i, kind):
        if i == 7:
            ref, device = wt.at[zof(i), y, half, lanes(0)], at(dx=(1, 3, 2)[kind])
        elif kind == 0:
            ref, device = wt.at[zof(i), y, half, lanes(0)], at(dy=1)
        elif kind == 1:
            ref, device = wt.at[zof(i), y, half, lanes(0)], at(dy=3)
        else:
            ref, device = wt.at[zof(i), y, half, lanes(0)], at(dy=2)
        return remote(ref, ref, y_s.at[i, kind], y_r.at[i, kind], device)

    def x_move(i, kind):
        if i == 7:
            row = (y + (0, 0, 3, 1)[kind]) % 4
            part = (pl.ds(0, HH), pl.ds(0, HH), pl.ds(0, HALF), pl.ds(HALF, HALF))[kind]
            ref, device = wt.at[zof(i), row, half, part], at(dy=(1, 3, 1, 3)[kind])
        elif kind == 0:
            ref, device = wt.at[zof(i), :, half, lanes(0)], at(dx=1)
        elif kind == 1:
            ref, device = wt.at[zof(i), :, half, lanes(0)], at(dx=3)
        elif kind == 2:
            ref, device = wt.at[zof(i), pl.ds(0, 2), half, lanes(3)], at(dx=1)
        else:
            ref, device = wt.at[zof(i), pl.ds(2, 2), half, lanes(1)], at(dx=3)
        return remote(ref, ref, x_s.at[i, kind], x_r.at[i, kind], device)

    def x_first(r, kind):
        row = (y + r) % 4
        if kind < 2:
            ref, device = wt.at[z, row, half, lanes(0)], at(dx=3 if kind else 1)
        elif r < 2:
            ref, device = wt.at[z, row, half, lanes(3)], at(dx=1)
        else:
            ref, device = wt.at[z, row, half, lanes(1)], at(dx=3)
        return remote(ref, ref, f_s.at[r, kind], f_r.at[r, kind], device)

    def last_mirror(n):
        if n < 5:
            rows = pl.ds(0, 2) if n == 3 else pl.ds(2, 2) if n == 4 else pl.ds(0, 4)
            ref = wt.at[zof(6), rows, half, lanes((0, 3, 1, 2, 2)[n])]
        else:
            ref = wt.at[zof(7), (y + (0, 3, 1, 2)[n - 5]) % 4, half]
        return remote(ref, ref, m_s.at[6 + n], m_r.at[6 + n], partner)

    def mirror(i):
        ref = wt.at[zof(i), :, half]
        return remote(ref, ref, m_s.at[i], m_r.at[i], partner)

    x_first(0, 0).start()
    x_first(0, 1).start()
    z_move(0, ("r", 0)).start()
    z_move(0, ("l", 0)).start()
    for kind in range(3):
        y_move(0, kind).start()
    def exchange(h):
        moves = []
        lane_half = pl.ds(h * HALF, HALF)
        for j, off in ((1, sigma), (2, 8 - 2 * sigma), (3, 3 * sigma + 8)):
            to_z = (z + off + 8) % 8
            for n, ref in enumerate((ck_ref, cv_ref)):
                src = ref.at[to_z // 2, :, lane_half]
                sems = cache_s.at[h, j, n], cache_r.at[h, j, n]
                moves.append(remote(src, cache.at[h, j, n], *sems, (to_z * 4 + y, f)))
        for d in range(1, 8):
            to = (me + d) % 8
            sems = qkv_s.at[h, d], qkv_r.at[h, d]
            moves.append(remote(send.at[h, to], recv.at[h, me], *sems, member(to)))
        own = [pltpu.make_async_copy(send.at[h, me], recv.at[h, me], loc.at[h, 1])]
        for n, ref in enumerate((ck_ref, cv_ref)):
            src = ref.at[z // 2, :, lane_half]
            own.append(pltpu.make_async_copy(src, cache.at[h, 0, n], loc.at[h, 2 + n]))
        return moves, own

    exchanges = [exchange(0), exchange(1)]

    def start_exchange(h):
        if h:
            for move in exchanges[0][0]:
                move.wait_send()
        for move in exchanges[h][0] + exchanges[h][1]:
            move.start()

    def spatial(first, count):
        @pl.loop(first, first + count)
        def _(h):
            cols = pl.ds(pl.multiple_of(h * HD, HD), HD)
            scores = lax.dot_general(q_ref[:, cols], k_ref[:, cols], NT, preferred_element_type=F32)
            weights, inverse = softmax_parts(scores * SCALE2 + near_ref[...])
            values = jnp.dot(weights, v_ref[:, cols], preferred_element_type=F32)
            mixed[:, cols] = (values * inverse).astype(BF16)

    def z_steps(i):
        k = (i + 1) // 2
        if i % 2:
            z_move(i, ("r", k - 1)).wait_recv()
            if k < 4:
                z_move(i, ("r", k)).start()
        else:
            z_move(i, ("l", k - 1)).wait_recv()
            if k < 3:
                z_move(i, ("l", k)).start()
        y_move(i, 0).start()
        y_move(i, 1).start()
        y_move(i, 2).start()

    def y_steps(i):
        for kind, r in enumerate((3, 1, 2)):
            y_move(i, kind).wait_recv()
            if i == 0:
                x_first(r, 0).start()
                x_first(r, 1).start()
        if i:
            x_move(i, 0).start()
            x_move(i, 1).start()

    def x_steps(i):
        if i == 0:
            for r in (0, 3, 1, 2):
                x_first(r, 0).wait_recv()
                if r < 2:
                    x_first(r, 2).start()
                x_first(r, 1).wait_recv()
                if r >= 2:
                    x_first(r, 2).start()
            return
        x_move(i, 0).wait_recv()
        x_move(i, 2).start()
        if i >= 6:
            last_mirror(1 if i == 6 else 6).start()
        x_move(i, 1).wait_recv()
        x_move(i, 3).start()
        if i >= 6:
            last_mirror(2 if i == 6 else 7).start()

    def x_last(i):
        if i == 0:
            for r in range(4):
                x_first(r, 2).wait_recv()
        elif i == 7:
            last_mirror(5).start()
            x_move(i, 2).wait_recv()
            x_move(i, 3).wait_recv()
            last_mirror(8).start()
            return
        elif i == 6:
            last_mirror(0).start()
            x_move(i, 2).wait_recv()
            last_mirror(3).start()
            x_move(i, 3).wait_recv()
            last_mirror(4).start()
            return
        else:
            x_move(i, 2).wait_recv()
            x_move(i, 3).wait_recv()
        mirror(i).start()

    def o_exchange(h):
        moves = []
        for d in range(1, 8):
            to = (me + d) % 8
            sems = o_s.at[h, d], o_r.at[h, d]
            moves.append(remote(o_send.at[h, to], o_recv.at[h, me], *sems, member(to)))
        return moves, pltpu.make_async_copy(o_send.at[h, me], o_recv.at[h, me], loc.at[h, 4])

    o_exchanges = [o_exchange(0), o_exchange(1)]

    def temporal(h):
        moves, own = exchanges[h]
        for move in own:
            move.wait()
        for move in moves:
            move.wait_recv()

        for p in range(2):
            rows = pl.ds(p * 16, 16)
            slots = pl.ds(p * 2, 2)

            def head(cols):
                queries = recv[h, :, 0, rows, cols].reshape(128, HD)
                span_k = recv[h, :, 1, rows, cols].reshape(128, HD)
                span_v = recv[h, :, 2, rows, cols].reshape(128, HD)
                old_k = cache[h, slots, 0, :, cols].reshape(128, HD)
                old_v = cache[h, slots, 1, :, cols].reshape(128, HD)
                keys = jnp.concatenate([span_k, old_k], axis=0)
                values = jnp.concatenate([span_v, old_v], axis=0)
                scores = lax.dot_general(queries, keys, NT, preferred_element_type=F32)
                weights, inverse = softmax_parts(scores * SCALE2 + live_ref[...])
                result = jnp.dot(weights, values, preferred_element_type=F32) * inverse
                o_send[h, :, rows, cols] = result.astype(BF16).reshape(8, 16, HD)

            @pl.loop(0, 10 // TEMPORAL_UNROLL)
            def _(step, head=head):
                for n in range(TEMPORAL_UNROLL):
                    head(pl.ds(pl.multiple_of((step * TEMPORAL_UNROLL + n) * HD, HD), HD))

        moves, own = o_exchanges[h]
        for move in moves:
            move.start()
        own.start()

    def combine(h):
        moves, own = o_exchanges[h]
        own.wait()
        for move in moves:
            move.wait_recv()

        for step in range(5):
            cols = pl.ds(step * 256, 256)
            to_cols = pl.ds(h * HALF + step * 256, 256)
            rows = jnp.dot(
                back_ref[...], o_recv[h, :, :, cols].reshape(256, 256), preferred_element_type=F32
            )
            mixed[:, to_cols] = (mixed[:, to_cols].astype(F32) + rows).astype(BF16)

    def out_move(i):
        cols = pl.ds(pl.multiple_of(zof(i) * 640, 128), 640)
        return pltpu.make_async_copy(out_buf.at[i % 2], out_ref.at[:, cols], out_s.at[i % 2])

    def project(i, h):
        lane_half = pl.ds(h * HALF, HALF)
        if h == 0 and i < 6:
            mirror(i).wait_recv()
        elif h == 0:
            for n in range(5) if i == 6 else range(5, 9):
                last_mirror(n).wait_recv()
        block = wt[zof(i), :, :, lane_half].reshape(640, HALF)
        result = lax.dot_general(mixed[:, lane_half], block, NT, preferred_element_type=F32)
        if h == 0:
            total[i] = result
        else:
            if i > 1:
                out_move(i - 2).wait()
            out_buf[i % 2] = (result + total[i]).astype(BF16)
            out_move(i).start()

    def run(step):
        kind, index = step[0], int(step[1:])
        if kind == "b":
            for move in staged:
                move.wait()
            tables(
                z, order_ref, near_tiles_ref, frames_ref, perm_ref, back_ref, near_ref, live_ref
            )
        elif kind == "z":
            z_steps(index)
        elif kind == "y":
            y_steps(index)
        elif kind == "x":
            x_steps(index)
        elif kind == "l":
            x_last(index)
        elif kind == "s":
            spatial(index * 4, 4)
        elif kind == "k":
            pack(index)
        elif kind == "a":
            start_exchange(index)
        elif kind == "t":
            temporal(index)
        elif kind == "c":
            combine(index)
        elif kind == "p":
            project(index % 10, index // 10)

    for step in SCHEDULE:
        run(step)
    out_move(6).wait()
    out_move(7).wait()

    for h in range(2):
        for move in (exchanges[h][0] if h else []) + o_exchanges[h][0]:
            move.wait_send()
    for k in range(4):
        z_move(0, ("r", k)).wait_send()
    for k in range(3):
        z_move(0, ("l", k)).wait_send()
    for i in range(8):
        for kind in range(3):
            y_move(i, kind).wait_send()
        for kind in range(4 if i else 0):
            x_move(i, kind).wait_send()
        if i < 6:
            mirror(i).wait_send()
    for r in range(4):
        for kind in range(3):
            x_first(r, kind).wait_send()
    for n in range(9):
        last_mirror(n).wait_send()


def shards(queries, key_rows, value_rows, cache_keys, cache_values, cache_frames, neighbors, tile_order, out_weight):
    vmem = pl.BlockSpec(memory_space=pltpu.VMEM)
    hbm = pl.BlockSpec(memory_space=pl.ANY)
    dma = pltpu.SemaphoreType.DMA
    out = pl.pallas_call(
        kernel,
        out_shape=jax.ShapeDtypeStruct((256, D), BF16),
        in_specs=[hbm] * 3 + [vmem] * 2 + [pl.BlockSpec(memory_space=pltpu.SMEM)] + [hbm] * 3,
        out_specs=hbm,
        scratch_shapes=[
            pltpu.VMEM((2, 8, 3, 32, HALF), BF16),
            pltpu.VMEM((2, 8, 3, 32, HALF), BF16),
            pltpu.VMEM((2, 4, 2, 64, HALF), BF16),
            pltpu.VMEM((2, 8, 32, HALF), BF16),
            pltpu.VMEM((2, 8, 32, HALF), BF16),
            pltpu.VMEM((256, HH), BF16),
            pltpu.VMEM((256, HH), BF16),
            pltpu.VMEM((256, HH), BF16),
            pltpu.VMEM((256, HH), BF16),
            pltpu.VMEM((256, 256), BF16),
            pltpu.VMEM((256, 256), BF16),
            pltpu.VMEM((256, 256), F32),
            pltpu.VMEM((128, 256), F32),
            pltpu.VMEM((2, 80, 320), BF16),
            pltpu.VMEM((8, 4, 160, HH), BF16),
            pltpu.VMEM((2, 256, 640), BF16),
            pltpu.VMEM((8, 256, 640), F32),
            dma((1,)),
            dma((1,)),
            dma((2, 5)),
            dma((2, 8)),
            dma((2, 8)),
            dma((2, 4, 2)),
            dma((2, 4, 2)),
            dma((2, 8)),
            dma((2, 8)),
            dma((8,)),
            dma((8,)),
            dma((8, 3)),
            dma((8, 3)),
            dma((8, 4)),
            dma((8, 4)),
            dma((4, 3)),
            dma((4, 3)),
            dma((15,)),
            dma((15,)),
            dma((2,)),
        ],
        compiler_params=pltpu.CompilerParams(
            collective_id=0, has_side_effects=True, vmem_limit_bytes=60 * 2**20
        ),
        cost_estimate=pl.CostEstimate(flops=9 * 10**9, bytes_accessed=2 * 10**7, transcendentals=3 * 10**6),
    )(
        queries.reshape(256, HH),
        key_rows.reshape(256, HH),
        value_rows.reshape(256, HH),
        tile_order.reshape(1, 32),
        neighbors.T,
        cache_frames.T,
        cache_keys.reshape(4, 64, HH),
        cache_values.reshape(4, 64, HH),
        out_weight.T,
    )
    return out.reshape(1, 1, 256, D)


def solution(mesh):
    placed = (
        P("seq", "fsdp", None, None),
        P("seq", "fsdp", None, None),
        P("seq", "fsdp", None, None),
        P("seq", None, "fsdp", None, None),
        P("seq", None, "fsdp", None, None),
        P(None, "fsdp"),
        P(),
        P(),
        P("fsdp", "seq"),
    )
    return jax.shard_map(
        shards, mesh=mesh, in_specs=placed, out_specs=P("seq", "fsdp", None, None), check_vma=False
    )
```
